512 devices in a mesh: pair: 64 (over y, z), ctr: 8 (over x, core).
Axes of the slice: x: 4, y: 8, z: 8, core: 2. Of those that a mesh axis runs over, the one named last changes fastest.
Arguments:
- amplitudes: bfloat16 [1536, 30720], P('pair', 'ctr'), may hold values from -6 to 6
- integrals: bfloat16 [32768, 30720], P('pair', 'ctr'), may hold values from -0.03125 to 0.03125
- block_size: int32 [64], replicated, may hold values from 1 to 24, 1024 in all
- block_owner: int32 [64], replicated, may hold values from 0 to 63, each once
Outputs:
- ladder: bfloat16 [1024, 32768], P('ctr', 'pair')
The draws below stay inside these ranges and needn't reach their ends.
Inputs may be any that keep to these rules, and one draw needn't show every extreme that they name: `block_size`: each block holds at least one occupied pair; the sizes sum to 1024 and the largest equals 24. `block_owner`: every owner holds exactly one block.
All inputs are finite; a program needn't handle non-finite values.
Results may differ from the reference program's by a relative error of at most 0.001.
Values may be sent and summed in bfloat16 or wider, within the bound.
A program may use at most 64 MiB of HBM per device.

```python
import math
import jax
import jax.numpy as jnp
import numpy as np
from jax import lax

CD = 30720
AB_DEV = 512
CAP = 24
IJ = 1024
SLOTS = 1536
AB = 32768
N_PAIR = 64


def levels(key, extent, shards, smallest, largest):
    factor_of = 1.0
    for position, parts in shards:
        draws = jax.random.uniform(jax.random.fold_in(jax.random.fold_in(key, 6), position), (parts,), jnp.float32, smallest / len(shards), largest / len(shards))
        factor_of = factor_of * jnp.repeat(jnp.exp(draws), extent[position] // parts).reshape((-1,) + (1,) * (len(extent) - 1 - position))
    return factor_of


def length_profile(count, total, limit, slope):
    weights = [(1 << 20) // math.isqrt(rank ** slope) + 1 for rank in range(2, count + 1)]
    spare, counts = total - limit - (count - 1), [1] * (count - 1)
    while spare > 0:
        movable = [i for i in range(count - 1) if counts[i] < limit]
        whole, budget = sum([weights[i] for i in movable]), spare
        for i in movable:
            more = min(limit - counts[i], max(1, budget * weights[i] // whole), spare)
            counts[i] = counts[i] + more
            spare = spare - more
    return np.array([limit] + counts)


def uneven(stream_key, count, total, limit, skew):
    if count == 2:
        one = jax.random.randint(stream_key, (), max(1, total - limit), min(limit, total - 1) + 1)
        return jnp.stack([one, total - one])
    lengths = jnp.asarray(length_profile(count, total, limit, skew), jnp.int32)
    pairs = (count - 1) // 2
    donor, sink = lengths[1:1 + 2 * pairs:2], lengths[2:2 + 2 * pairs:2]
    slack = jnp.minimum(donor - 1, limit - sink)
    moved = jax.random.randint(jax.random.fold_in(stream_key, 1), (pairs,), 0, 1 << 20) % (slack + 1)
    lengths = lengths.at[1:1 + 2 * pairs:2].set(donor - moved).at[2:2 + 2 * pairs:2].set(sink + moved)
    return lengths[jax.random.permutation(jax.random.fold_in(stream_key, 2), count)]


def gaussian(stream_key, dims, deviation, limit, cuts=(), kind=jnp.bfloat16):
    entries = deviation * jax.random.normal(stream_key, dims, jnp.float32)
    if cuts:
        entries = entries * levels(stream_key, dims, cuts, -0.22, 0.18)
    return jnp.clip(entries, -limit, limit).astype(kind)


def setup_inputs(seed: int = 0) -> dict:
    keys = jax.random.split(jax.random.key(seed), 5)
    return {
        "amplitudes": gaussian(keys[0], (SLOTS, CD), 1.0, 6.0, ((0, 64), (1, 8))),
        "integrals": gaussian(keys[1], (AB, CD), CD ** -0.5, 0.03125, ((0, 64), (1, 8))),
        "block_size": uneven(keys[2], N_PAIR, IJ, CAP, 2).astype(jnp.int32),
        "block_owner": jax.random.permutation(keys[3], N_PAIR).astype(jnp.int32),
    }


def find_sources(block_size, block_owner, total_rows, slot_count):
    ending = jnp.cumsum(block_size).astype(jnp.int32)
    block_offset = (ending - block_size).astype(jnp.int32)
    row_ids = jnp.arange(total_rows, dtype=jnp.int32)
    block_ids = jnp.sum((row_ids[:, None] >= ending[None, :]).astype(jnp.int32), axis=1).astype(jnp.int32)
    one_hot = (block_ids[:, None] == jnp.arange(block_size.shape[0], dtype=jnp.int32)[None, :]).astype(jnp.int32)
    first_row = jnp.sum(one_hot * block_offset[None, :], axis=1).astype(jnp.int32)
    owner_ids = jnp.sum(one_hot * block_owner[None, :], axis=1).astype(jnp.int32)
    return (owner_ids * slot_count + row_ids - first_row).astype(jnp.int32)


def reference(amplitudes, integrals, block_size, block_owner):
    sources = find_sources(block_size, block_owner, IJ, CAP)
    canonical = jnp.take(amplitudes, sources, axis=0)
    blocked = integrals.reshape(N_PAIR, AB_DEV, CD)

    def one_block(rows_ab):
        return lax.dot_general(canonical, rows_ab, (((1,), (1,)), ((), ())), preferred_element_type=jnp.float32)

    products = lax.map(one_block, blocked)
    ladder = jnp.transpose(products, (1, 0, 2)).reshape(IJ, N_PAIR * AB_DEV)
    return ladder.astype(jnp.bfloat16)
```

```python
import functools

import jax
import jax.numpy as jnp
import numpy as np
from jax import lax
from jax.experimental import pallas as pl
from jax.experimental.pallas import tpu as pltpu
from jax.sharding import PartitionSpec as P

MESH = pl.DeviceIdType.MESH
NY = 8
NZ = 8
NX = 4
CAP = 24
SUB = 2
OFFS = (0, -1, 1, -2, 2, -3, 3, -4)
GROUPS = ((0, 2), (2, 6), (6, 8))


def ring_distance(d):
    d = d % 8
    return min(d, 8 - d)


def order_tables():
    first, second, names = [], [], []
    for delta in range(8):
        order = sorted(range(8), key=lambda o: (max(ring_distance(o), ring_distance(o - delta)), o))
        done = [max(ring_distance(o), ring_distance(o - delta)) for o in order]
        assert done[1] <= 2 and done[5] <= 3
        first.append(sum(order.index(OFFS[s] % 8) * 8**s for s in range(8)))
        second.append(sum(order.index((delta + OFFS[s]) % 8) * 8**s for s in range(8)))
        names.append(sum(order[i] * 8**i for i in range(8)))
    return first, second, names


def pick(table, delta):
    total = 0
    for d in range(8):
        total = total + table[d] * (1 - lax.div(lax.rem(delta - d + 8, 8) + 7, 8))
    return total


def digit(packed, i):
    return lax.rem(lax.div(packed, 8**i), 8)


def iota(shape, dim):
    return lax.broadcasted_iota(jnp.int32, shape, dim)


def kernel(
    a_ref, b_hbm, size_ref, owner_ref, out_ref,
    msg, got, sel, blocks, b_ref, acc, from_core, sums, from_x, final,
    b_sem, send0, recv0, send1, recv1, send2, recv2, send_c, recv_c, send_x, recv_x,
):
    pair = lax.axis_index("pair")
    ctr = lax.axis_index("ctr")
    y, z = lax.div(pair, NZ), lax.rem(pair, NZ)
    x, core = lax.div(ctr, 2), lax.rem(ctr, 2)
    delta = lax.rem(y - z + 8, 8)
    half = a_ref.shape[1] // 2
    piece = got.shape[-1]
    parts = half // piece

    def along(axis, d):
        if axis == "y":
            return (lax.rem(y + d + NY, NY) * NZ + z, ctr)
        return (y * NZ + lax.rem(z + d + NZ, NZ), ctr)

    other_core = (pair, ctr + 1 - 2 * core)

    def along_x(d):
        return (pair, lax.rem(x + d, NX) * 2 + core)

    loads = []
    for h in range(2):
        load = pltpu.make_async_copy(b_hbm.at[:, pl.ds(h * half, half)], b_ref.at[h], b_sem.at[h])
        load.start()
        loads.append(load)

    barrier = pltpu.get_barrier_semaphore()
    peers = [along("y", d) for d in range(1, 8)] + [along("z", d) for d in range(1, 8)]
    peers += [other_core] + [along_x(d) for d in range(1, 4)]
    for peer in peers:
        pl.semaphore_signal(barrier, inc=1, device_id=peer, device_id_type=MESH)

    sends = []

    def send(src, dst, send_sem, recv_sem, device):
        copy = pltpu.make_async_remote_copy(
            src_ref=src, dst_ref=dst, send_sem=send_sem, recv_sem=recv_sem,
            device_id=device, device_id_type=MESH,
        )
        copy.start()
        sends.append(copy)
        return copy

    size_row = size_ref[...].astype(jnp.float32)
    owner_row = owner_ref[...].astype(jnp.float32)
    n_block = size_row.shape[1]
    rows, cols = iota((n_block, n_block), 0), iota((n_block, n_block), 1)
    zero = jnp.zeros((n_block, n_block), jnp.float32)
    size_col = jnp.sum(jnp.where(rows == cols, size_row + zero, 0.0), axis=1, keepdims=True)
    owner_col = jnp.sum(jnp.where(rows == cols, owner_row + zero, 0.0), axis=1, keepdims=True)
    offset_col = jnp.sum(jnp.where(cols < rows, size_row + zero, 0.0), axis=1, keepdims=True)

    mine = owner_col == pair.astype(jnp.float32)
    my_offset = jnp.sum(jnp.where(mine, offset_col, 0.0), axis=0, keepdims=True).astype(jnp.int32)
    n_msg = 8 * 16
    at = iota((n_msg, CAP), 0)
    slot = iota((n_msg, CAP), 1)
    wanted = jnp.where(
        ((slot + my_offset) & 7) == (at >> 4), (at & 15) - parts * (slot >> 3), -1
    )
    for h in range(2):
        total = jnp.zeros((n_msg, piece), jnp.float32)
        for q in range(parts):
            choose = jnp.where(wanted == q, 1.0, 0.0).astype(jnp.bfloat16)
            total += jnp.dot(
                choose, a_ref[:, h * half + q * piece : h * half + (q + 1) * piece],
                preferred_element_type=jnp.float32,
            )
        msg[h] = total.astype(jnp.bfloat16).reshape(8, 16, piece)

    pl.semaphore_wait(barrier, len(peers))

    phase0 = []
    for d in range(1, 8):
        for h, axis, me in ((0, "z", z), (1, "y", y)):
            phase0.append(
                send(
                    msg.at[h, lax.rem(me + d, 8)], got.at[h, 0, me],
                    send0.at[h, d - 1], recv0.at[h, d - 1], along(axis, d),
                )
            )
    got[0, 0, z] = msg[0, z]
    got[1, 0, y] = msg[1, y]

    width = got.shape[1] * n_msg
    place = iota((1, width), 1)
    slot_of = place >> 7
    source = (place >> 4) & 7
    m = place & 15
    i = jnp.where(m >= parts, 1, 0) + jnp.where(m >= 2 * parts, 1, 0) + jnp.where(m >= 3 * parts, 1, 0)
    q = m - parts * i
    step = (slot_of + 1) >> 1
    ring = jnp.where((slot_of & 1) == 0, step, 8 - step)

    for h in range(2):
        if h == 0:
            owner = ((ring + y) & 7) * NZ + source
            cls = z
        else:
            owner = source * NZ + ((ring + z) & 7)
            cls = y
        hit = owner_col == owner.astype(jnp.float32)
        first = jnp.sum(jnp.where(hit, offset_col, 0.0), axis=0, keepdims=True).astype(jnp.int32)
        count = jnp.sum(jnp.where(hit, size_col, 0.0), axis=0, keepdims=True).astype(jnp.int32)
        k = ((first - cls + 7) >> 3) + i
        good = (8 * k + cls < first + count) & (i < 3)
        target = q * 128 + ((k >> 4) & 1) * 64 + (k >> 5) * 16 + (k & 15)
        target = jnp.where(good, target, -1)

        def fill(part, carry, h=h, target=target):
            row = iota((128, width), 0) + part * 128
            sel[h, part] = jnp.where(row == target, 1.0, 0.0).astype(jnp.bfloat16)
            return carry

        lax.fori_loop(0, parts, fill, 0)

    for copy in phase0:
        copy.wait_recv()

    def ring_sends(buf, h, axis, step, u, n_sub, send_sem, recv_sem):
        started = []
        for way in range(2):
            if step == 3 and (u < n_sub // 2) != (way == 0):
                continue
            src = 0 if step == 0 else 2 * step - 1 + way
            dst = 7 if step == 3 else 2 * step + 1 + way
            rows_of = buf.shape[2] // n_sub
            at_rows = pl.ds(u * rows_of, rows_of)
            started.append(
                send(
                    buf.at[h, src, at_rows], buf.at[h, dst, at_rows],
                    send_sem.at[h, way, step, u], recv_sem.at[h, way, step, u],
                    along(axis, 1 if way == 0 else -1),
                )
            )
        return started

    acc[...] = jnp.zeros_like(acc)
    lanes = (("y", "z"), ("z", "y"))

    def first_ring(step):
        out = []
        for h in range(2):
            for u in range(2):
                if step < 3:
                    if u == 0:
                        out += ring_sends(got, h, lanes[h][0], step, 0, 1, send1, recv1)
                else:
                    out += ring_sends(got, h, lanes[h][0], step, u, 2, send1, recv1)
        return out

    flying = first_ring(0)
    for step in range(1, 4):
        for copy in flying:
            copy.wait_recv()
        flying = first_ring(step)
    for copy in flying:
        copy.wait_recv()

    landed = {}

    def second_ring(step, h, u):
        landed[step, h, u] = ring_sends(blocks, h, lanes[h][1], step, u, SUB, send2, recv2)

    for h in range(2):
        packed = got[h].reshape(width, piece)
        for part in range(parts):
            value = jnp.dot(sel[h, part], packed, preferred_element_type=jnp.float32)
            blocks[h, 0, :, part * piece : (part + 1) * piece] = value.astype(jnp.bfloat16)
        for u in range(SUB):
            second_ring(0, h, u)

    first_table, second_table, name_table = order_tables()
    where_to = (pick(first_table, delta), pick(second_table, delta))
    names = pick(name_table, delta)

    def multiply(slot0, n_slot):
        for h in range(2):
            left = blocks[h, slot0 : slot0 + n_slot].reshape(n_slot * 128, half)
            value = lax.dot_general(
                left, b_ref[h], (((1,), (1,)), ((), ())), preferred_element_type=jnp.float32
            )
            for s in range(n_slot):
                pos = digit(where_to[h], slot0 + s)
                for c in range(2):
                    acc[c, pos] += value[s * 128 + c * 64 : s * 128 + c * 64 + 64]

    def arrive(step):
        for u in range(SUB):
            for h in range(2):
                for copy in landed[step, h, u]:
                    copy.wait_recv()
                if step < 3:
                    second_ring(step + 1, h, u)

    def core_send(g):
        lo, hi = GROUPS[g]
        return send(
            acc.at[1 - core, pl.ds(lo, hi - lo)], from_core.at[pl.ds(lo, hi - lo)],
            send_c.at[g], recv_c.at[g], other_core,
        )

    def x_send(g, exchanged):
        lo, hi = GROUPS[g]
        exchanged.wait_recv()
        for t in range(NX):
            sums[t, lo:hi] = acc[core, lo:hi, t * 16 : t * 16 + 16] + from_core[lo:hi, t * 16 : t * 16 + 16]
        return [
            send(
                sums.at[lax.rem(x + d, NX), pl.ds(lo, hi - lo)], from_x.at[d - 1, pl.ds(lo, hi - lo)],
                send_x.at[g, d - 1], recv_x.at[g, d - 1], along_x(d),
            )
            for d in range(1, NX)
        ]

    def finish(g, copies):
        lo, hi = GROUPS[g]
        for copy in copies:
            copy.wait_recv()
        value = sums[x, lo:hi] + from_x[0, lo:hi] + from_x[1, lo:hi] + from_x[2, lo:hi]
        final[lo:hi] = value.astype(jnp.bfloat16)

    for load in loads:
        load.wait()
    multiply(0, 1)
    arrive(0)
    multiply(1, 2)
    arrive(1)
    multiply(3, 2)
    core_a = core_send(0)
    arrive(2)
    x_a = x_send(0, core_a)
    multiply(5, 2)
    core_b = core_send(1)
    x_b = x_send(1, core_b)
    arrive(3)
    multiply(7, 1)
    core_c = core_send(2)
    row, col = iota((128, 128), 0), iota((128, 128), 1)
    pos = col >> 4
    cls = jnp.zeros((128, 128), jnp.int32)
    for n in range(8):
        cls = jnp.where(pos == n, lax.rem(digit(names, n) + z, 8), cls)
    order = jnp.where(row == (col & 15) * 8 + cls, 1.0, 0.0).astype(jnp.bfloat16)
    x_c = x_send(2, core_c)
    finish(0, x_a)
    finish(1, x_b)
    finish(2, x_c)
    value = jnp.dot(order, final[...].reshape(128, final.shape[-1]), preferred_element_type=jnp.float32)
    out_ref[...] = value.astype(jnp.bfloat16)
    for copy in sends:
        copy.wait_send()


def on_device(amplitudes, integrals, block_size, block_owner):
    slots, depth = amplitudes.shape
    ab = integrals.shape[0]
    half = depth // 2
    piece = half // 5
    n_blocks = block_size.shape[0]
    vmem = pl.BlockSpec(memory_space=pltpu.VMEM)
    dma = pltpu.SemaphoreType.DMA
    return pl.pallas_call(
        kernel,
        out_shape=jax.ShapeDtypeStruct((128, ab), jnp.bfloat16),
        in_specs=[vmem, pl.BlockSpec(memory_space=pl.ANY), vmem, vmem],
        out_specs=vmem,
        scratch_shapes=[
            pltpu.VMEM((2, 8, 16, piece), jnp.bfloat16),
            pltpu.VMEM((2, 8, 8, 16, piece), jnp.bfloat16),
            pltpu.VMEM((2, 5, 128, 1024), jnp.bfloat16),
            pltpu.VMEM((2, 8, 128, half), jnp.bfloat16),
            pltpu.VMEM((2, ab, half), jnp.bfloat16),
            pltpu.VMEM((2, 8, 64, ab), jnp.float32),
            pltpu.VMEM((8, 64, ab), jnp.float32),
            pltpu.VMEM((NX, 8, 16, ab), jnp.float32),
            pltpu.VMEM((NX - 1, 8, 16, ab), jnp.float32),
            pltpu.VMEM((8, 16, ab), jnp.bfloat16),
            dma((2,)),
            dma((2, 7)),
            dma((2, 7)),
            dma((2, 2, 4, 2)),
            dma((2, 2, 4, 2)),
            dma((2, 2, 4, SUB)),
            dma((2, 2, 4, SUB)),
            dma((3,)),
            dma((3,)),
            dma((3, NX - 1)),
            dma((3, NX - 1)),
        ],
        compiler_params=pltpu.CompilerParams(
            collective_id=0, has_side_effects=True, vmem_limit_bytes=50 * 1024 * 1024
        ),
        cost_estimate=pl.CostEstimate(
            flops=2 * 1024 * ab * depth, bytes_accessed=2 * ab * depth, transcendentals=0
        ),
    )(
        amplitudes,
        integrals,
        block_size.reshape(1, n_blocks),
        block_owner.reshape(1, n_blocks),
    )


def solution(mesh):
    in_specs = (P("pair", "ctr"), P("pair", "ctr"), P(), P())
    return jax.shard_map(
        on_device, mesh=mesh, in_specs=in_specs, out_specs=P("ctr", "pair"), check_vma=False
    )
```

```python
import functools

import jax
import jax.numpy as jnp
import numpy as np
from jax import lax
from jax.experimental import pallas as pl
from jax.experimental.pallas import tpu as pltpu
from jax.sharding import PartitionSpec as P

MESH = pl.DeviceIdType.MESH
NY = 8
NZ = 8
NX = 4
CAP = 24
PIECES = 3
OFFS = (0, -1, 1, -2, 2, -3, 3, -4)
GROUPS = ((0, 2), (2, 6), (6, 8))


def ring_distance(d):
    d = d % 8
    return min(d, 8 - d)


def order_tables():
    first, second, names = [], [], []
    for delta in range(8):
        order = sorted(range(8), key=lambda o: (max(ring_distance(o), ring_distance(o - delta)), o))
        done = [max(ring_distance(o), ring_distance(o - delta)) for o in order]
        assert done[1] <= 2 and done[5] <= 3
        first.append(sum(order.index(OFFS[s] % 8) * 8**s for s in range(8)))
        second.append(sum(order.index((delta + OFFS[s]) % 8) * 8**s for s in range(8)))
        names.append(sum(order[i] * 8**i for i in range(8)))
    return first, second, names


def pick(table, delta):
    total = 0
    for d in range(8):
        total = total + table[d] * (1 - lax.div(lax.rem(delta - d + 8, 8) + 7, 8))
    return total


def digit(packed, i):
    return lax.rem(lax.div(packed, 8**i), 8)


def iota(shape, dim):
    return lax.broadcasted_iota(jnp.int32, shape, dim)


def kernel(
    a_hbm, b_hbm, size_hbm, owner_hbm, out_ref,
    a_ref, size_ref, owner_ref, msg, got, sel, blocks, b_ref, acc, from_core, sums, from_x, final,
    in_sem, b_sem, send0, recv0, send1, recv1, send2, recv2, send_c, recv_c, send_x, recv_x,
):
    pair = lax.axis_index("pair")
    ctr = lax.axis_index("ctr")
    y, z = lax.div(pair, NZ), lax.rem(pair, NZ)
    x, core = lax.div(ctr, 2), lax.rem(ctr, 2)
    delta = lax.rem(y - z + 8, 8)
    half = a_ref.shape[1] // 2
    lane = got.shape[-1]
    piece = half // PIECES
    parts = piece // lane

    def along(axis, d):
        if axis == "y":
            return (lax.rem(y + d + NY, NY) * NZ + z, ctr)
        return (y * NZ + lax.rem(z + d + NZ, NZ), ctr)

    other_core = (pair, ctr + 1 - 2 * core)

    def along_x(d):
        return (pair, lax.rem(x + d, NX) * 2 + core)

    inputs = []
    for n, (src, dst) in enumerate(((size_hbm, size_ref), (owner_hbm, owner_ref), (a_hbm, a_ref))):
        load = pltpu.make_async_copy(src, dst, in_sem.at[n])
        load.start()
        inputs.append(load)

    barrier = pltpu.get_barrier_semaphore()
    peers = [along("y", d) for d in range(1, 8)] + [along("z", d) for d in range(1, 8)]
    peers += [other_core] + [along_x(d) for d in range(1, 4)]
    for peer in peers:
        pl.semaphore_signal(barrier, inc=1, device_id=peer, device_id_type=MESH)

    for load in inputs:
        load.wait()
    loads = []
    for h in range(2):
        load = pltpu.make_async_copy(b_hbm.at[:, pl.ds(h * half, half)], b_ref.at[h], b_sem.at[h])
        load.start()
        loads.append(load)

    sends = []

    def send(src, dst, send_sem, recv_sem, device):
        copy = pltpu.make_async_remote_copy(
            src_ref=src, dst_ref=dst, send_sem=send_sem, recv_sem=recv_sem,
            device_id=device, device_id_type=MESH,
        )
        copy.start()
        sends.append(copy)
        return copy

    size_row = size_ref[...].astype(jnp.float32)
    owner_row = owner_ref[...].astype(jnp.float32)
    n_block = size_row.shape[1]
    rows, cols = iota((n_block, n_block), 0), iota((n_block, n_block), 1)
    zero = jnp.zeros((n_block, n_block), jnp.float32)
    size_col = jnp.sum(jnp.where(rows == cols, size_row + zero, 0.0), axis=1, keepdims=True)
    owner_col = jnp.sum(jnp.where(rows == cols, owner_row + zero, 0.0), axis=1, keepdims=True)
    offset_col = jnp.sum(jnp.where(cols < rows, size_row + zero, 0.0), axis=1, keepdims=True)

    mine = owner_col == pair.astype(jnp.float32)
    my_offset = jnp.sum(jnp.where(mine, offset_col, 0.0), axis=0, keepdims=True).astype(jnp.int32)
    n_msg = 8 * 16
    at = iota((n_msg, CAP), 0)
    slot = iota((n_msg, CAP), 1)
    wanted = jnp.where(
        ((slot + my_offset) & 7) == (at >> 4), (at & 15) - parts * (slot >> 3), -1
    )
    choose = [jnp.where(wanted == q, 1.0, 0.0).astype(jnp.bfloat16) for q in range(parts)]
    for h in range(2):
        for a in range(PIECES):
            total = jnp.zeros((n_msg, lane), jnp.float32)
            for q in range(parts):
                start = h * half + a * piece + q * lane
                total += jnp.dot(
                    choose[q], a_ref[:, start : start + lane], preferred_element_type=jnp.float32
                )
            msg[h, a] = total.astype(jnp.bfloat16).reshape(8, 16, lane)

    pl.semaphore_wait(barrier, len(peers))

    phase0 = []
    for d in range(1, 8):
        for h, axis, me in ((0, "z", z), (1, "y", y)):
            phase0.append(
                send(
                    msg.at[h, :, lax.rem(me + d, 8)], got.at[h, :, 0, me],
                    send0.at[h, d - 1], recv0.at[h, d - 1], along(axis, d),
                )
            )
    for a in range(PIECES):
        got[0, a, 0, z] = msg[0, a, z]
        got[1, a, 0, y] = msg[1, a, y]

    width = got.shape[2] * n_msg
    place = iota((1, width), 1)
    slot_of = place >> 7
    source = (place >> 4) & 7
    m = place & 15
    i = jnp.where(m >= parts, 1, 0) + jnp.where(m >= 2 * parts, 1, 0) + jnp.where(m >= 3 * parts, 1, 0)
    q = m - parts * i
    step = (slot_of + 1) >> 1
    ring = jnp.where((slot_of & 1) == 0, step, 8 - step)

    targets = []
    for h in range(2):
        if h == 0:
            owner = ((ring + y) & 7) * NZ + source
            cls = z
        else:
            owner = source * NZ + ((ring + z) & 7)
            cls = y
        hit = owner_col == owner.astype(jnp.float32)
        first = jnp.sum(jnp.where(hit, offset_col, 0.0), axis=0, keepdims=True).astype(jnp.int32)
        count = jnp.sum(jnp.where(hit, size_col, 0.0), axis=0, keepdims=True).astype(jnp.int32)
        k = ((first - cls + 7) >> 3) + i
        good = (8 * k + cls < first + count) & (i < 3)
        target = q * 128 + ((k >> 4) & 1) * 64 + (k >> 5) * 16 + (k & 15)
        targets.append(jnp.where(good, target, -1))

    def select(h):
        def fill(part, carry):
            row = iota((128, width), 0) + part * 128
            sel[h, pl.ds(part * 128, 128)] = jnp.where(row == targets[h], 1.0, 0.0).astype(jnp.bfloat16)
            return carry

        lax.fori_loop(0, parts, fill, 0)

    for copy in phase0:
        copy.wait_recv()

    lanes = (("y", "z"), ("z", "y"))

    def ring_send(view, n_rows, h, a, way, step, send_sem, recv_sem, axis):
        src = 0 if step == 0 else 2 * step - 1 + way
        dst = 7 if step == 3 else 2 * step + 1 + way
        rows = pl.ds(0, n_rows) if step < 3 else pl.ds(way * (n_rows // 2), n_rows // 2)
        return send(
            view(h, a, src, rows), view(h, a, dst, rows),
            send_sem.at[h, way, step, a], recv_sem.at[h, way, step, a],
            along(axis, 1 if way == 0 else -1),
        )

    flying1, flying2 = {}, {}

    def first_ring(step, a, h, way):
        flying1[step, a, h, way] = ring_send(
            lambda h, a, slot, rows: got.at[h, a, slot, rows], 8,
            h, a, way, step, send1, recv1, lanes[h][0],
        )

    def second_ring(step, a, h, way):
        flying2[step, a, h, way] = ring_send(
            lambda h, a, slot, rows: blocks.at[h, slot, rows, pl.ds(a * piece, piece)], 128,
            h, a, way, step, send2, recv2, lanes[h][1],
        )

    both = [(h, way) for way in range(2) for h in range(2)]
    for a in range(PIECES):
        for h, way in both:
            first_ring(0, a, h, way)
    select(0)
    acc[...] = jnp.zeros_like(acc)
    for step in range(3):
        for a in range(PIECES):
            for h, way in both:
                flying1[step, a, h, way].wait_recv()
                first_ring(step + 1, a, h, way)
        if step == 0:
            select(1)

    for a in range(PIECES):
        for h in range(2):
            for way in range(2):
                flying1[3, a, h, way].wait_recv()
            value = jnp.dot(
                sel[h], got[h, a].reshape(width, lane), preferred_element_type=jnp.float32
            ).astype(jnp.bfloat16)
            for q in range(parts):
                start = a * piece + q * lane
                blocks[h, 0, :, start : start + lane] = value[q * 128 : q * 128 + 128]
            for way in range(2):
                second_ring(0, a, h, way)

    first_table, second_table, name_table = order_tables()
    where_to = (pick(first_table, delta), pick(second_table, delta))
    names = pick(name_table, delta)

    def multiply(slot0, n_slot, a):
        for h in range(2):
            columns = pl.ds(a * piece, piece)
            left = blocks[h, slot0 : slot0 + n_slot, :, columns].reshape(n_slot * 128, piece)
            value = lax.dot_general(
                left, b_ref[h, :, columns], (((1,), (1,)), ((), ())), preferred_element_type=jnp.float32
            )
            for s in range(n_slot):
                pos = digit(where_to[h], slot0 + s)
                for c in range(2):
                    acc[c, pos] += value[s * 128 + c * 64 : s * 128 + c * 64 + 64]

    def arrive(step, a):
        for h, way in both:
            flying2[step, a, h, way].wait_recv()
            if step < 3:
                second_ring(step + 1, a, h, way)

    def core_send(g):
        lo, hi = GROUPS[g]
        return send(
            acc.at[1 - core, pl.ds(lo, hi - lo)], from_core.at[pl.ds(lo, hi - lo)],
            send_c.at[g], recv_c.at[g], other_core,
        )

    def x_send(g, exchanged):
        lo, hi = GROUPS[g]
        exchanged.wait_recv()
        for t in range(NX):
            sums[t, lo:hi] = acc[core, lo:hi, t * 16 : t * 16 + 16] + from_core[lo:hi, t * 16 : t * 16 + 16]
        return [
            send(
                sums.at[lax.rem(x + d, NX), pl.ds(lo, hi - lo)], from_x.at[d - 1, pl.ds(lo, hi - lo)],
                send_x.at[g, d - 1], recv_x.at[g, d - 1], along_x(d),
            )
            for d in range(1, NX)
        ]

    def finish(g, copies):
        lo, hi = GROUPS[g]
        for copy in copies:
            copy.wait_recv()
        value = sums[x, lo:hi] + from_x[0, lo:hi] + from_x[1, lo:hi] + from_x[2, lo:hi]
        final[lo:hi] = value.astype(jnp.bfloat16)

    for load in loads:
        load.wait()
    for a in range(PIECES):
        multiply(0, 1, a)
    for step in range(2):
        for a in range(PIECES):
            arrive(step, a)
            multiply(2 * step + 1, 2, a)
    core_a = core_send(0)
    for a in range(PIECES):
        arrive(2, a)
        if a == 0:
            x_a = x_send(0, core_a)
        multiply(5, 2, a)
    core_b = core_send(1)
    for a in range(PIECES):
        arrive(3, a)
        if a == 0:
            x_b = x_send(1, core_b)
        multiply(7, 1, a)
    core_c = core_send(2)
    row, col = iota((128, 128), 0), iota((128, 128), 1)
    pos = col >> 4
    cls = jnp.zeros((128, 128), jnp.int32)
    for n in range(8):
        cls = jnp.where(pos == n, lax.rem(digit(names, n) + z, 8), cls)
    order = jnp.where(row == (col & 15) * 8 + cls, 1.0, 0.0).astype(jnp.bfloat16)
    x_c = x_send(2, core_c)
    finish(0, x_a)
    finish(1, x_b)
    finish(2, x_c)
    value = jnp.dot(order, final[...].reshape(128, final.shape[-1]), preferred_element_type=jnp.float32)
    out_ref[...] = value.astype(jnp.bfloat16)
    for copy in sends:
        copy.wait_send()


def on_device(amplitudes, integrals, block_size, block_owner):
    slots, depth = amplitudes.shape
    ab = integrals.shape[0]
    half = depth // 2
    lane = half // PIECES // 5
    n_blocks = block_size.shape[0]
    vmem = pl.BlockSpec(memory_space=pltpu.VMEM)
    dma = pltpu.SemaphoreType.DMA
    return pl.pallas_call(
        kernel,
        out_shape=jax.ShapeDtypeStruct((128, ab), jnp.bfloat16),
        in_specs=[pl.BlockSpec(memory_space=pltpu.HBM)] * 4,
        out_specs=vmem,
        scratch_shapes=[
            pltpu.VMEM((slots, depth), jnp.bfloat16),
            pltpu.VMEM((1, n_blocks), jnp.int32),
            pltpu.VMEM((1, n_blocks), jnp.int32),
            pltpu.VMEM((2, PIECES, 8, 16, lane), jnp.bfloat16),
            pltpu.VMEM((2, PIECES, 8, 8, 16, lane), jnp.bfloat16),
            pltpu.VMEM((2, 5 * 128, 8 * 128), jnp.bfloat16),
            pltpu.VMEM((2, 8, 128, half), jnp.bfloat16),
            pltpu.VMEM((2, ab, half), jnp.bfloat16),
            pltpu.VMEM((2, 8, 64, ab), jnp.float32),
            pltpu.VMEM((8, 64, ab), jnp.float32),
            pltpu.VMEM((NX, 8, 16, ab), jnp.float32),
            pltpu.VMEM((NX - 1, 8, 16, ab), jnp.float32),
            pltpu.VMEM((8, 16, ab), jnp.bfloat16),
            dma((3,)),
            dma((2,)),
            dma((2, 7)),
            dma((2, 7)),
            dma((2, 2, 4, PIECES)),
            dma((2, 2, 4, PIECES)),
            dma((2, 2, 4, PIECES)),
            dma((2, 2, 4, PIECES)),
            dma((3,)),
            dma((3,)),
            dma((3, NX - 1)),
            dma((3, NX - 1)),
        ],
        compiler_params=pltpu.CompilerParams(
            collective_id=0, has_side_effects=True, vmem_limit_bytes=60 * 1024 * 1024
        ),
        cost_estimate=pl.CostEstimate(
            flops=2 * 1024 * ab * depth, bytes_accessed=2 * ab * depth, transcendentals=0
        ),
    )(
        amplitudes,
        integrals,
        block_size.reshape(1, n_blocks),
        block_owner.reshape(1, n_blocks),
    )


def solution(mesh):
    in_specs = (P("pair", "ctr"), P("pair", "ctr"), P(), P())
    return jax.shard_map(
        on_device, mesh=mesh, in_specs=in_specs, out_specs=P("ctr", "pair"), check_vma=False
    )
```

```python
import functools

import jax
import jax.numpy as jnp
import numpy as np
from jax import lax
from jax.experimental import pallas as pl
from jax.experimental.pallas import tpu as pltpu
from jax.sharding import PartitionSpec as P

MESH = pl.DeviceIdType.MESH
NY = 8
NZ = 8
NX = 4
CAP = 24
PIECES = 3
OFFS = (0, -1, 1, -2, 2, -3, 3, -4)
GROUPS = ((0, 2), (2, 6), (6, 8))


def ring_distance(d):
    d = d % 8
    return min(d, 8 - d)


def order_tables():
    first, second, names = [], [], []
    for delta in range(8):
        order = sorted(range(8), key=lambda o: (max(ring_distance(o), ring_distance(o - delta)), o))
        done = [max(ring_distance(o), ring_distance(o - delta)) for o in order]
        assert done[1] <= 2 and done[5] <= 3
        first.append(sum(order.index(OFFS[s] % 8) * 8**s for s in range(8)))
        second.append(sum(order.index((delta + OFFS[s]) % 8) * 8**s for s in range(8)))
        names.append(sum(order[i] * 8**i for i in range(8)))
    return first, second, names


def pick(table, delta):
    total = 0
    for d in range(8):
        total = total + table[d] * (1 - lax.div(lax.rem(delta - d + 8, 8) + 7, 8))
    return total


def digit(packed, i):
    return lax.rem(lax.div(packed, 8**i), 8)


def iota(shape, dim):
    return lax.broadcasted_iota(jnp.int32, shape, dim)


def kernel(
    a_hbm, b_hbm, size_hbm, owner_hbm, out_ref,
    a_ref, size_ref, owner_ref, msg, got, sel, blocks, b_ref, acc, early, from_core, sums, from_opposite, from_x, final,
    in_sem, b_sem, send0, recv0, send1, recv1, send2, recv2, send_c, recv_c, send_o, recv_o, send_x, recv_x,
):
    pair = lax.axis_index("pair")
    ctr = lax.axis_index("ctr")
    y, z = lax.div(pair, NZ), lax.rem(pair, NZ)
    x, core = lax.div(ctr, 2), lax.rem(ctr, 2)
    delta = lax.rem(y - z + 8, 8)
    half = a_ref.shape[1] // 2
    lane = got.shape[-1]
    piece = half // PIECES
    parts = piece // lane

    def along(axis, d):
        if axis == "y":
            return (lax.rem(y + d + NY, NY) * NZ + z, ctr)
        return (y * NZ + lax.rem(z + d + NZ, NZ), ctr)

    other_core = (pair, ctr + 1 - 2 * core)

    def along_x(d):
        return (pair, lax.rem(x + d, NX) * 2 + core)

    inputs = []
    for n, (src, dst) in enumerate(((size_hbm, size_ref), (owner_hbm, owner_ref), (a_hbm, a_ref))):
        load = pltpu.make_async_copy(src, dst, in_sem.at[n])
        load.start()
        inputs.append(load)

    barrier = pltpu.get_barrier_semaphore()
    peers = [along("y", d) for d in range(1, 8)] + [along("z", d) for d in range(1, 8)]
    peers += [other_core] + [along_x(1), along_x(3)]
    for peer in peers:
        pl.semaphore_signal(barrier, inc=1, device_id=peer, device_id_type=MESH)

    sends = []

    def send(src, dst, send_sem, recv_sem, device):
        copy = pltpu.make_async_remote_copy(
            src_ref=src, dst_ref=dst, send_sem=send_sem, recv_sem=recv_sem,
            device_id=device, device_id_type=MESH,
        )
        copy.start()
        sends.append(copy)
        return copy

    def drain(count):
        for copy in sends[:count]:
            copy.wait_send()
        del sends[:count]

    inputs[0].wait()
    inputs[1].wait()
    size_row = size_ref[...].astype(jnp.float32)
    owner_row = owner_ref[...].astype(jnp.float32)
    n_block = size_row.shape[1]
    rows, cols = iota((n_block, n_block), 0), iota((n_block, n_block), 1)
    zero = jnp.zeros((n_block, n_block), jnp.float32)
    size_col = jnp.sum(jnp.where(rows == cols, size_row + zero, 0.0), axis=1, keepdims=True)
    owner_col = jnp.sum(jnp.where(rows == cols, owner_row + zero, 0.0), axis=1, keepdims=True)
    offset_col = jnp.sum(jnp.where(cols < rows, size_row + zero, 0.0), axis=1, keepdims=True)

    mine = owner_col == pair.astype(jnp.float32)
    my_offset = jnp.sum(jnp.where(mine, offset_col, 0.0), axis=0, keepdims=True).astype(jnp.int32)
    n_msg = 8 * 16
    at = iota((n_msg, CAP), 0)
    slot = iota((n_msg, CAP), 1)
    wanted = jnp.where(
        ((slot + my_offset) & 7) == (at >> 4), (at & 15) - parts * (slot >> 3), -1
    )
    choose = [jnp.where(wanted == q, 1.0, 0.0).astype(jnp.bfloat16) for q in range(parts)]
    inputs[2].wait()
    loads = []
    for h in range(2):
        load = pltpu.make_async_copy(b_hbm.at[:, pl.ds(h * half, half)], b_ref.at[h], b_sem.at[h])
        load.start()
        loads.append(load)

    for h in range(2):
        for a in range(PIECES):
            total = jnp.zeros((n_msg, lane), jnp.float32)
            for q in range(parts):
                start = h * half + a * piece + q * lane
                total += jnp.dot(
                    choose[q], a_ref[:, start : start + lane], preferred_element_type=jnp.float32
                )
            msg[h, a] = total.astype(jnp.bfloat16).reshape(8, 16, lane)

    pl.semaphore_wait(barrier, len(peers))

    phase0 = []
    for d in range(1, 8):
        for h, axis, me in ((0, "z", z), (1, "y", y)):
            phase0.append(
                send(
                    msg.at[h, :, lax.rem(me + d, 8)], got.at[h, :, 0, me],
                    send0.at[h, d - 1], recv0.at[h, d - 1], along(axis, d),
                )
            )
    for a in range(PIECES):
        got[0, a, 0, z] = msg[0, a, z]
        got[1, a, 0, y] = msg[1, a, y]

    width = got.shape[2] * n_msg
    place = iota((1, width), 1)
    slot_of = place >> 7
    source = (place >> 4) & 7
    m = place & 15
    i = jnp.where(m >= parts, 1, 0) + jnp.where(m >= 2 * parts, 1, 0) + jnp.where(m >= 3 * parts, 1, 0)
    q = m - parts * i
    step = (slot_of + 1) >> 1
    ring = jnp.where((slot_of & 1) == 0, step, 8 - step)

    targets = []
    for h in range(2):
        if h == 0:
            owner = ((ring + y) & 7) * NZ + source
            cls = z
        else:
            owner = source * NZ + ((ring + z) & 7)
            cls = y
        hit = owner_col == owner.astype(jnp.float32)
        first = jnp.sum(jnp.where(hit, offset_col, 0.0), axis=0, keepdims=True).astype(jnp.int32)
        count = jnp.sum(jnp.where(hit, size_col, 0.0), axis=0, keepdims=True).astype(jnp.int32)
        k = ((first - cls + 7) >> 3) + i
        good = (8 * k + cls < first + count) & (i < 3)
        target = q * 128 + ((k >> 4) & 1) * 64 + (k >> 5) * 16 + (k & 15)
        targets.append(jnp.where(good, target, -1))

    def select(h):
        def fill(part, carry):
            row = iota((128, width), 0) + part * 128
            sel[h, pl.ds(part * 128, 128)] = jnp.where(row == targets[h], 1.0, 0.0).astype(jnp.bfloat16)
            return carry

        lax.fori_loop(0, parts, fill, 0)

    for copy in phase0:
        copy.wait_recv()

    lanes = (("y", "z"), ("z", "y"))

    def ring_send(view, n_rows, h, a, way, step, send_sem, recv_sem, axis):
        src = 0 if step == 0 else 2 * step - 1 + way
        dst = 7 if step == 3 else 2 * step + 1 + way
        rows = pl.ds(0, n_rows) if step < 3 else pl.ds(way * (n_rows // 2), n_rows // 2)
        return send(
            view(h, a, src, rows), view(h, a, dst, rows),
            send_sem.at[h, way, step, a], recv_sem.at[h, way, step, a],
            along(axis, 1 if way == 0 else -1),
        )

    flying1, flying2 = {}, {}

    def first_ring(step, a, h, way):
        flying1[step, a, h, way] = ring_send(
            lambda h, a, slot, rows: got.at[h, a, slot, rows], 8,
            h, a, way, step, send1, recv1, lanes[h][0],
        )

    def second_ring(step, a, h, way):
        flying2[step, a, h, way] = ring_send(
            lambda h, a, slot, rows: blocks.at[h, slot, rows, pl.ds(a * piece, piece)], 128,
            h, a, way, step, send2, recv2, lanes[h][1],
        )

    both = [(h, way) for way in range(2) for h in range(2)]
    for a in range(PIECES):
        for h, way in both:
            first_ring(0, a, h, way)
    select(0)
    acc[...] = jnp.zeros_like(acc)
    for step in range(3):
        for a in range(PIECES):
            for h, way in both:
                flying1[step, a, h, way].wait_recv()
                first_ring(step + 1, a, h, way)
        if step == 0:
            select(1)
        if step == 1:
            for h in range(2):
                early[h] = jnp.dot(
                    sel[h, :, : 5 * n_msg], got[h, 0, :5].reshape(5 * n_msg, lane),
                    preferred_element_type=jnp.float32,
                )

    n_early = len(sends)

    for a in range(PIECES):
        for h in range(2):
            for way in range(2):
                flying1[3, a, h, way].wait_recv()
            if a == 0:
                value = early[h] + jnp.dot(
                    sel[h, :, 5 * n_msg :], got[h, 0, 5:].reshape(3 * n_msg, lane),
                    preferred_element_type=jnp.float32,
                )
            else:
                value = jnp.dot(
                    sel[h], got[h, a].reshape(width, lane), preferred_element_type=jnp.float32
                )
            value = value.astype(jnp.bfloat16)
            for q in range(parts):
                start = a * piece + q * lane
                blocks[h, 0, :, start : start + lane] = value[q * 128 : q * 128 + 128]
            for way in range(2):
                second_ring(0, a, h, way)

    first_table, second_table, name_table = order_tables()
    where_to = (pick(first_table, delta), pick(second_table, delta))
    names = pick(name_table, delta)

    def multiply(slot0, n_slot, a):
        for h in range(2):
            columns = pl.ds(a * piece, piece)
            left = blocks[h, slot0 : slot0 + n_slot, :, columns].reshape(n_slot * 128, piece)
            value = lax.dot_general(
                left, b_ref[h, :, columns], (((1,), (1,)), ((), ())), preferred_element_type=jnp.float32
            )
            for s in range(n_slot):
                pos = digit(where_to[h], slot0 + s)
                for c in range(2):
                    acc[c, pos] += value[s * 128 + c * 64 : s * 128 + c * 64 + 64]

    def arrive(step, a):
        for h, way in both:
            flying2[step, a, h, way].wait_recv()
            if step < 3:
                second_ring(step + 1, a, h, way)

    def core_send(g):
        lo, hi = GROUPS[g]
        return send(
            acc.at[1 - core, pl.ds(lo, hi - lo)], from_core.at[pl.ds(lo, hi - lo)],
            send_c.at[g], recv_c.at[g], other_core,
        )

    right, left, opposite = (lax.rem(x + d, NX) for d in (1, 3, 2))

    def x_first(g, exchanged):
        lo, hi = GROUPS[g]
        exchanged.wait_recv()
        for t in range(NX):
            sums[t, lo:hi] = acc[core, lo:hi, t * 16 : t * 16 + 16] + from_core[lo:hi, t * 16 : t * 16 + 16]
        return [
            send(
                sums.at[opposite, pl.ds(lo, hi - lo), pl.ds(w * 8, 8)], from_opposite.at[w, pl.ds(lo, hi - lo)],
                send_o.at[g, w], recv_o.at[g, w], along_x((1, 3)[w]),
            )
            for w in range(2)
        ]

    def x_second(g, copies):
        lo, hi = GROUPS[g]
        out = []
        for w, near in ((0, right), (1, left)):
            copies[w].wait_recv()
            sums[near, lo:hi, w * 8 : w * 8 + 8] += from_opposite[w, lo:hi]
            out.append(
                send(
                    sums.at[near, pl.ds(lo, hi - lo)], from_x.at[w, pl.ds(lo, hi - lo)],
                    send_x.at[g, w], recv_x.at[g, w], along_x((1, 3)[w]),
                )
            )
        return out

    def finish(g, copies):
        lo, hi = GROUPS[g]
        for copy in copies:
            copy.wait_recv()
        value = sums[x, lo:hi] + from_x[0, lo:hi] + from_x[1, lo:hi]
        final[lo:hi] = value.astype(jnp.bfloat16)

    for load in loads:
        load.wait()
    for a in range(PIECES):
        multiply(0, 1, a)
    for step in range(2):
        for a in range(PIECES):
            arrive(step, a)
            multiply(2 * step + 1, 2, a)
            if step == 0 and a == 0:
                drain(n_early)
    core_a = core_send(0)
    n_early = len(sends)
    for a in range(PIECES):
        arrive(2, a)
        if a == 0:
            x_a = x_first(0, core_a)
        if a == 1:
            x_a = x_second(0, x_a)
        multiply(5, 2, a)
    core_b = core_send(1)
    for a in range(PIECES):
        arrive(3, a)
        if a == 0:
            x_b = x_first(1, core_b)
        multiply(7, 1, a)
        if a == 1:
            x_b = x_second(1, x_b)
            drain(n_early)
            finish(0, x_a)
    core_c = core_send(2)
    row, col = iota((128, 128), 0), iota((128, 128), 1)
    pos = col >> 4
    cls = jnp.zeros((128, 128), jnp.int32)
    for n in range(8):
        cls = jnp.where(pos == n, lax.rem(digit(names, n) + z, 8), cls)
    order = jnp.where(row == (col & 15) * 8 + cls, 1.0, 0.0).astype(jnp.bfloat16)
    x_c = x_second(2, x_first(2, core_c))
    finish(1, x_b)
    drain(len(sends) - 4)
    finish(2, x_c)
    value = jnp.dot(order, final[...].reshape(128, final.shape[-1]), preferred_element_type=jnp.float32)
    out_ref[...] = value.astype(jnp.bfloat16)
    drain(len(sends))


def on_device(amplitudes, integrals, block_size, block_owner):
    slots, depth = amplitudes.shape
    ab = integrals.shape[0]
    half = depth // 2
    lane = half // PIECES // 5
    n_blocks = block_size.shape[0]
    vmem = pl.BlockSpec(memory_space=pltpu.VMEM)
    dma = pltpu.SemaphoreType.DMA
    return pl.pallas_call(
        kernel,
        out_shape=jax.ShapeDtypeStruct((128, ab), jnp.bfloat16),
        in_specs=[pl.BlockSpec(memory_space=pltpu.HBM)] * 4,
        out_specs=vmem,
        scratch_shapes=[
            pltpu.VMEM((slots, depth), jnp.bfloat16),
            pltpu.VMEM((1, n_blocks), jnp.int32),
            pltpu.VMEM((1, n_blocks), jnp.int32),
            pltpu.VMEM((2, PIECES, 8, 16, lane), jnp.bfloat16),
            pltpu.VMEM((2, PIECES, 8, 8, 16, lane), jnp.bfloat16),
            pltpu.VMEM((2, 5 * 128, 8 * 128), jnp.bfloat16),
            pltpu.VMEM((2, 8, 128, half), jnp.bfloat16),
            pltpu.VMEM((2, ab, half), jnp.bfloat16),
            pltpu.VMEM((2, 8, 64, ab), jnp.float32),
            pltpu.VMEM((2, 5 * 128, lane), jnp.float32),
            pltpu.VMEM((8, 64, ab), jnp.float32),
            pltpu.VMEM((NX, 8, 16, ab), jnp.float32),
            pltpu.VMEM((2, 8, 8, ab), jnp.float32),
            pltpu.VMEM((2, 8, 16, ab), jnp.float32),
            pltpu.VMEM((8, 16, ab), jnp.bfloat16),
            dma((3,)),
            dma((2,)),
            dma((2, 7)),
            dma((2, 7)),
            dma((2, 2, 4, PIECES)),
            dma((2, 2, 4, PIECES)),
            dma((2, 2, 4, PIECES)),
            dma((2, 2, 4, PIECES)),
            dma((3,)),
            dma((3,)),
            dma((3, 2)),
            dma((3, 2)),
            dma((3, 2)),
            dma((3, 2)),
        ],
        compiler_params=pltpu.CompilerParams(
            collective_id=0, has_side_effects=True, vmem_limit_bytes=60 * 1024 * 1024
        ),
        cost_estimate=pl.CostEstimate(
            flops=2 * 1024 * ab * depth, bytes_accessed=2 * ab * depth, transcendentals=0
        ),
    )(
        amplitudes,
        integrals,
        block_size.reshape(1, n_blocks),
        block_owner.reshape(1, n_blocks),
    )


def solution(mesh):
    in_specs = (P("pair", "ctr"), P("pair", "ctr"), P(), P())
    return jax.shard_map(
        on_device, mesh=mesh, in_specs=in_specs, out_specs=P("ctr", "pair"), check_vma=False
    )
```

```python
import functools

import jax
import jax.numpy as jnp
import numpy as np
from jax import lax
from jax.experimental import pallas as pl
from jax.experimental.pallas import tpu as pltpu
from jax.sharding import PartitionSpec as P

MESH = pl.DeviceIdType.MESH
NY = 8
NZ = 8
NX = 4
CAP = 24
PIECES = 3
OFFS = (0, -1, 1, -2, 2, -3, 3, -4)
GROUPS = ((0, 2), (2, 6), (6, 8))


def ring_distance(d):
    d = d % 8
    return min(d, 8 - d)


def order_tables():
    first, second, names = [], [], []
    for delta in range(8):
        order = sorted(range(8), key=lambda o: (max(ring_distance(o), ring_distance(o - delta)), o))
        done = [max(ring_distance(o), ring_distance(o - delta)) for o in order]
        assert done[1] <= 2 and done[5] <= 3
        first.append(sum(order.index(OFFS[s] % 8) * 8**s for s in range(8)))
        second.append(sum(order.index((delta + OFFS[s]) % 8) * 8**s for s in range(8)))
        names.append(sum(order[i] * 8**i for i in range(8)))
    return first, second, names


def pick(table, delta):
    total = 0
    for d in range(8):
        total = total + table[d] * (1 - lax.div(lax.rem(delta - d + 8, 8) + 7, 8))
    return total


def digit(packed, i):
    return lax.rem(lax.div(packed, 8**i), 8)


def iota(shape, dim):
    return lax.broadcasted_iota(jnp.int32, shape, dim)


def kernel(
    a_hbm, b_hbm, size_hbm, owner_hbm, out_ref,
    a_ref, size_ref, owner_ref, msg, got, sel, blocks, b_ref, acc, turned, early, from_core, sums, from_opposite, from_x, final,
    in_sem, b_sem, send0, recv0, send1, recv1, send2, recv2, send_c, recv_c, send_o, recv_o, send_x, recv_x,
):
    pair = lax.axis_index("pair")
    ctr = lax.axis_index("ctr")
    y, z = lax.div(pair, NZ), lax.rem(pair, NZ)
    x, core = lax.div(ctr, 2), lax.rem(ctr, 2)
    delta = lax.rem(y - z + 8, 8)
    half = a_ref.shape[1] // 2
    lane = got.shape[-1]
    piece = half // PIECES
    parts = piece // lane

    def along(axis, d):
        if axis == "y":
            return (lax.rem(y + d + NY, NY) * NZ + z, ctr)
        return (y * NZ + lax.rem(z + d + NZ, NZ), ctr)

    other_core = (pair, ctr + 1 - 2 * core)

    def along_x(d):
        return (pair, lax.rem(x + d, NX) * 2 + core)

    inputs = []
    for n, (src, dst) in enumerate(((size_hbm, size_ref), (owner_hbm, owner_ref), (a_hbm, a_ref))):
        load = pltpu.make_async_copy(src, dst, in_sem.at[n])
        load.start()
        inputs.append(load)

    barrier = pltpu.get_barrier_semaphore()
    peers = [along("y", d) for d in range(1, 8)] + [along("z", d) for d in range(1, 8)]
    peers += [other_core] + [along_x(1), along_x(3)]
    for peer in peers:
        pl.semaphore_signal(barrier, inc=1, device_id=peer, device_id_type=MESH)

    sends = []

    def send(src, dst, send_sem, recv_sem, device):
        copy = pltpu.make_async_remote_copy(
            src_ref=src, dst_ref=dst, send_sem=send_sem, recv_sem=recv_sem,
            device_id=device, device_id_type=MESH,
        )
        copy.start()
        sends.append(copy)
        return copy

    def drain(count):
        for copy in sends[:count]:
            copy.wait_send()
        del sends[:count]

    inputs[0].wait()
    inputs[1].wait()
    size_row = size_ref[...].astype(jnp.float32)
    owner_row = owner_ref[...].astype(jnp.float32)
    n_block = size_row.shape[1]
    rows, cols = iota((n_block, n_block), 0), iota((n_block, n_block), 1)
    zero = jnp.zeros((n_block, n_block), jnp.float32)
    size_col = jnp.sum(jnp.where(rows == cols, size_row + zero, 0.0), axis=1, keepdims=True)
    owner_col = jnp.sum(jnp.where(rows == cols, owner_row + zero, 0.0), axis=1, keepdims=True)
    offset_col = jnp.sum(jnp.where(cols < rows, size_row + zero, 0.0), axis=1, keepdims=True)

    mine = owner_col == pair.astype(jnp.float32)
    my_offset = jnp.sum(jnp.where(mine, offset_col, 0.0), axis=0, keepdims=True).astype(jnp.int32)
    n_msg = 8 * 16
    at = iota((n_msg, CAP), 0)
    slot = iota((n_msg, CAP), 1)
    wanted = jnp.where(
        ((slot + my_offset) & 7) == (at >> 4), (at & 15) - parts * (slot >> 3), -1
    )
    choose = [jnp.where(wanted == q, 1.0, 0.0).astype(jnp.bfloat16) for q in range(parts)]
    inputs[2].wait()
    loads = []
    for h in range(2):
        load = pltpu.make_async_copy(b_hbm.at[:, pl.ds(h * half, half)], b_ref.at[h], b_sem.at[h])
        load.start()
        loads.append(load)

    for h in range(2):
        for a in range(PIECES):
            total = jnp.zeros((n_msg, lane), jnp.float32)
            for q in range(parts):
                start = h * half + a * piece + q * lane
                total += jnp.dot(
                    choose[q], a_ref[:, start : start + lane], preferred_element_type=jnp.float32
                )
            msg[h, a] = total.astype(jnp.bfloat16).reshape(8, 16, lane)

    pl.semaphore_wait(barrier, len(peers))

    phase0 = []
    for d in range(1, 8):
        for h, axis, me in ((0, "z", z), (1, "y", y)):
            phase0.append(
                send(
                    msg.at[h, :, lax.rem(me + d, 8)], got.at[h, :, 0, me],
                    send0.at[h, d - 1], recv0.at[h, d - 1], along(axis, d),
                )
            )
    for a in range(PIECES):
        got[0, a, 0, z] = msg[0, a, z]
        got[1, a, 0, y] = msg[1, a, y]

    width = got.shape[2] * n_msg
    place = iota((1, width), 1)
    slot_of = place >> 7
    source = (place >> 4) & 7
    m = place & 15
    i = jnp.where(m >= parts, 1, 0) + jnp.where(m >= 2 * parts, 1, 0) + jnp.where(m >= 3 * parts, 1, 0)
    q = m - parts * i
    step = (slot_of + 1) >> 1
    ring = jnp.where((slot_of & 1) == 0, step, 8 - step)

    targets = []
    for h in range(2):
        if h == 0:
            owner = ((ring + y) & 7) * NZ + source
            cls = z
        else:
            owner = source * NZ + ((ring + z) & 7)
            cls = y
        hit = owner_col == owner.astype(jnp.float32)
        first = jnp.sum(jnp.where(hit, offset_col, 0.0), axis=0, keepdims=True).astype(jnp.int32)
        count = jnp.sum(jnp.where(hit, size_col, 0.0), axis=0, keepdims=True).astype(jnp.int32)
        k = ((first - cls + 7) >> 3) + i
        good = (8 * k + cls < first + count) & (i < 3)
        target = q * 128 + ((k >> 4) & 1) * 64 + (k >> 5) * 16 + (k & 15)
        targets.append(jnp.where(good, target, -1))

    def select(h):
        def fill(part, carry):
            row = iota((128, width), 0) + part * 128
            sel[h, pl.ds(part * 128, 128)] = jnp.where(row == targets[h], 1.0, 0.0).astype(jnp.bfloat16)
            return carry

        lax.fori_loop(0, parts, fill, 0)

    for copy in phase0:
        copy.wait_recv()

    lanes = (("y", "z"), ("z", "y"))

    def ring_send(view, n_rows, h, a, way, step, send_sem, recv_sem, axis):
        src = 0 if step == 0 else 2 * step - 1 + way
        dst = 7 if step == 3 else 2 * step + 1 + way
        rows = pl.ds(0, n_rows) if step < 3 else pl.ds(way * (n_rows // 2), n_rows // 2)
        return send(
            view(h, a, src, rows), view(h, a, dst, rows),
            send_sem.at[h, way, step, a], recv_sem.at[h, way, step, a],
            along(axis, 1 if way == 0 else -1),
        )

    flying1, flying2 = {}, {}

    def first_ring(step, a, h, way):
        flying1[step, a, h, way] = ring_send(
            lambda h, a, slot, rows: got.at[h, a, slot, rows], 8,
            h, a, way, step, send1, recv1, lanes[h][0],
        )

    def second_ring(step, a, h, way):
        flying2[step, a, h, way] = ring_send(
            lambda h, a, slot, rows: blocks.at[h, slot, a, rows], piece,
            h, a, way, step, send2, recv2, lanes[h][1],
        )

    both = [(h, way) for way in range(2) for h in range(2)]
    for a in range(PIECES):
        for h, way in both:
            first_ring(0, a, h, way)
    select(0)
    acc[...] = jnp.zeros_like(acc)
    for step in range(3):
        for a in range(PIECES):
            for h, way in both:
                flying1[step, a, h, way].wait_recv()
                first_ring(step + 1, a, h, way)
        if step == 0:
            select(1)
        if step == 1:
            for h in range(2):
                early[h] = jnp.dot(
                    sel[h, :, : 5 * n_msg], got[h, 0, :5].reshape(5 * n_msg, lane),
                    preferred_element_type=jnp.float32,
                )

    n_early = len(sends)

    for a in range(PIECES):
        for h in range(2):
            for way in range(2):
                flying1[3, a, h, way].wait_recv()
            if a == 0:
                value = early[h] + jnp.dot(
                    sel[h, :, 5 * n_msg :], got[h, 0, 5:].reshape(3 * n_msg, lane),
                    preferred_element_type=jnp.float32,
                )
            else:
                value = jnp.dot(
                    sel[h], got[h, a].reshape(width, lane), preferred_element_type=jnp.float32
                )
            for q in range(parts):
                columns = value[q * 128 : q * 128 + 128].T
                blocks[h, 0, a, q * lane : q * lane + lane] = columns.astype(jnp.bfloat16)
            for way in range(2):
                second_ring(0, a, h, way)

    first_table, second_table, name_table = order_tables()
    where_to = (pick(first_table, delta), pick(second_table, delta))
    names = pick(name_table, delta)

    def multiply(slot0, n_slot, a):
        for h in range(2):
            columns = jnp.concatenate([blocks[h, slot0 + s, a] for s in range(n_slot)], axis=1)
            value = jnp.dot(
                b_ref[h, :, a * piece : a * piece + piece], columns, preferred_element_type=jnp.float32
            )
            for s in range(n_slot):
                acc[digit(where_to[h], slot0 + s)] += value[:, s * 128 : s * 128 + 128]

    def arrive(step, a):
        for h, way in both:
            flying2[step, a, h, way].wait_recv()
            if step < 3:
                second_ring(step + 1, a, h, way)

    def core_send(g):
        lo, hi = GROUPS[g]
        for pos in range(lo, hi):
            value = acc[pos].T
            for c in range(2):
                turned[c, pos] = value[c * 64 : c * 64 + 64]
        return send(
            turned.at[1 - core, pl.ds(lo, hi - lo)], from_core.at[pl.ds(lo, hi - lo)],
            send_c.at[g], recv_c.at[g], other_core,
        )

    right, left, opposite = (lax.rem(x + d, NX) for d in (1, 3, 2))

    def x_first(g, exchanged):
        lo, hi = GROUPS[g]
        exchanged.wait_recv()
        for t in range(NX):
            sums[t, lo:hi] = turned[core, lo:hi, t * 16 : t * 16 + 16] + from_core[lo:hi, t * 16 : t * 16 + 16]
        return [
            send(
                sums.at[opposite, pl.ds(lo, hi - lo), pl.ds(w * 8, 8)], from_opposite.at[w, pl.ds(lo, hi - lo)],
                send_o.at[g, w], recv_o.at[g, w], along_x((1, 3)[w]),
            )
            for w in range(2)
        ]

    def x_second(g, copies):
        lo, hi = GROUPS[g]
        out = []
        for w, near in ((0, right), (1, left)):
            copies[w].wait_recv()
            sums[near, lo:hi, w * 8 : w * 8 + 8] += from_opposite[w, lo:hi]
            out.append(
                send(
                    sums.at[near, pl.ds(lo, hi - lo)], from_x.at[w, pl.ds(lo, hi - lo)],
                    send_x.at[g, w], recv_x.at[g, w], along_x((1, 3)[w]),
                )
            )
        return out

    def finish(g, copies):
        lo, hi = GROUPS[g]
        for copy in copies:
            copy.wait_recv()
        value = sums[x, lo:hi] + from_x[0, lo:hi] + from_x[1, lo:hi]
        final[lo:hi] = value.astype(jnp.bfloat16)

    for load in loads:
        load.wait()
    for a in range(PIECES):
        multiply(0, 1, a)
    for step in range(2):
        for a in range(PIECES):
            arrive(step, a)
            multiply(2 * step + 1, 2, a)
            if step == 0 and a == 0:
                drain(n_early)
    core_a = core_send(0)
    n_early = len(sends)
    for a in range(PIECES):
        arrive(2, a)
        if a == 0:
            x_a = x_first(0, core_a)
        if a == 1:
            x_a = x_second(0, x_a)
        multiply(5, 2, a)
    core_b = core_send(1)
    for a in range(PIECES):
        arrive(3, a)
        if a == 0:
            x_b = x_first(1, core_b)
        multiply(7, 1, a)
        if a == 1:
            x_b = x_second(1, x_b)
            drain(n_early)
            finish(0, x_a)
    core_c = core_send(2)
    row, col = iota((128, 128), 0), iota((128, 128), 1)
    pos = col >> 4
    cls = jnp.zeros((128, 128), jnp.int32)
    for n in range(8):
        cls = jnp.where(pos == n, lax.rem(digit(names, n) + z, 8), cls)
    order = jnp.where(row == (col & 15) * 8 + cls, 1.0, 0.0).astype(jnp.bfloat16)
    x_c = x_second(2, x_first(2, core_c))
    finish(1, x_b)
    drain(len(sends) - 4)
    finish(2, x_c)
    value = jnp.dot(order, final[...].reshape(128, final.shape[-1]), preferred_element_type=jnp.float32)
    out_ref[...] = value.astype(jnp.bfloat16)
    drain(len(sends))


def on_device(amplitudes, integrals, block_size, block_owner):
    slots, depth = amplitudes.shape
    ab = integrals.shape[0]
    half = depth // 2
    lane = half // PIECES // 5
    n_blocks = block_size.shape[0]
    vmem = pl.BlockSpec(memory_space=pltpu.VMEM)
    dma = pltpu.SemaphoreType.DMA
    return pl.pallas_call(
        kernel,
        out_shape=jax.ShapeDtypeStruct((128, ab), jnp.bfloat16),
        in_specs=[pl.BlockSpec(memory_space=pltpu.HBM)] * 4,
        out_specs=vmem,
        scratch_shapes=[
            pltpu.VMEM((slots, depth), jnp.bfloat16),
            pltpu.VMEM((1, n_blocks), jnp.int32),
            pltpu.VMEM((1, n_blocks), jnp.int32),
            pltpu.VMEM((2, PIECES, 8, 16, lane), jnp.bfloat16),
            pltpu.VMEM((2, PIECES, 8, 8, 16, lane), jnp.bfloat16),
            pltpu.VMEM((2, 5 * 128, 8 * 128), jnp.bfloat16),
            pltpu.VMEM((2, 8, PIECES, half // PIECES, 128), jnp.bfloat16),
            pltpu.VMEM((2, ab, half), jnp.bfloat16),
            pltpu.VMEM((8, ab, 128), jnp.float32),
            pltpu.VMEM((2, 8, 64, ab), jnp.float32),
            pltpu.VMEM((2, 5 * 128, lane), jnp.float32),
            pltpu.VMEM((8, 64, ab), jnp.float32),
            pltpu.VMEM((NX, 8, 16, ab), jnp.float32),
            pltpu.VMEM((2, 8, 8, ab), jnp.float32),
            pltpu.VMEM((2, 8, 16, ab), jnp.float32),
            pltpu.VMEM((8, 16, ab), jnp.bfloat16),
            dma((3,)),
            dma((2,)),
            dma((2, 7)),
            dma((2, 7)),
            dma((2, 2, 4, PIECES)),
            dma((2, 2, 4, PIECES)),
            dma((2, 2, 4, PIECES)),
            dma((2, 2, 4, PIECES)),
            dma((3,)),
            dma((3,)),
            dma((3, 2)),
            dma((3, 2)),
            dma((3, 2)),
            dma((3, 2)),
        ],
        compiler_params=pltpu.CompilerParams(
            collective_id=0, has_side_effects=True, vmem_limit_bytes=60 * 1024 * 1024
        ),
        cost_estimate=pl.CostEstimate(
            flops=2 * 1024 * ab * depth, bytes_accessed=2 * ab * depth, transcendentals=0
        ),
    )(
        amplitudes,
        integrals,
        block_size.reshape(1, n_blocks),
        block_owner.reshape(1, n_blocks),
    )


def solution(mesh):
    in_specs = (P("pair", "ctr"), P("pair", "ctr"), P(), P())
    return jax.shard_map(
        on_device, mesh=mesh, in_specs=in_specs, out_specs=P("ctr", "pair"), check_vma=False
    )
```

```python
import functools

import jax
import jax.numpy as jnp
import numpy as np
from jax import lax
from jax.experimental import pallas as pl
from jax.experimental.pallas import tpu as pltpu
from jax.sharding import PartitionSpec as P

MESH = pl.DeviceIdType.MESH
NY = 8
NZ = 8
NX = 4
CAP = 24
PIECES = 6
OFFS = (0, -1, 1, -2, 2, -3, 3, -4)
GROUPS = ((0, 2), (2, 6), (6, 8))


def ring_distance(d):
    d = d % 8
    return min(d, 8 - d)


def order_tables():
    first, second, names = [], [], []
    for delta in range(8):
        order = sorted(range(8), key=lambda o: (max(ring_distance(o), ring_distance(o - delta)), o))
        done = [max(ring_distance(o), ring_distance(o - delta)) for o in order]
        assert done[1] <= 2 and done[5] <= 3
        first.append(sum(order.index(OFFS[s] % 8) * 8**s for s in range(8)))
        second.append(sum(order.index((delta + OFFS[s]) % 8) * 8**s for s in range(8)))
        names.append(sum(order[i] * 8**i for i in range(8)))
    return first, second, names


def pick(table, delta):
    total = 0
    for d in range(8):
        total = total + table[d] * (1 - lax.div(lax.rem(delta - d + 8, 8) + 7, 8))
    return total


def digit(packed, i):
    return lax.rem(lax.div(packed, 8**i), 8)


def iota(shape, dim):
    return lax.broadcasted_iota(jnp.int32, shape, dim)


def kernel(
    a_hbm, b_hbm, size_hbm, owner_hbm, out_ref,
    a_ref, size_ref, owner_ref, msg, got, sel, blocks, b_ref, acc, early, from_core, sums, from_opposite, from_x, final,
    in_sem, b_sem, send0, recv0, send1, recv1, send2, recv2, send_c, recv_c, send_o, recv_o, send_x, recv_x,
):
    pair = lax.axis_index("pair")
    ctr = lax.axis_index("ctr")
    y, z = lax.div(pair, NZ), lax.rem(pair, NZ)
    x, core = lax.div(ctr, 2), lax.rem(ctr, 2)
    delta = lax.rem(y - z + 8, 8)
    lane = got.shape[-1]
    piece = a_ref.shape[1] // PIECES
    parts = piece // lane
    me = z + (y - z) * core
    me_before = y + (z - y) * core

    def along(d):
        return (lax.rem(y + d * core + NY, NY) * NZ + lax.rem(z + d * (1 - core) + NZ, NZ), ctr)

    def along_before(d):
        return (lax.rem(y + d * (1 - core) + NY, NY) * NZ + lax.rem(z + d * core + NZ, NZ), ctr)

    other_core = (pair, ctr + 1 - 2 * core)

    def along_x(d):
        return (pair, lax.rem(x + d, NX) * 2 + core)

    inputs = []
    for n, (src, dst) in enumerate(((size_hbm, size_ref), (owner_hbm, owner_ref), (a_hbm, a_ref))):
        load = pltpu.make_async_copy(src, dst, in_sem.at[n])
        load.start()
        inputs.append(load)

    barrier = pltpu.get_barrier_semaphore()
    peers = [along(d) for d in range(1, 8)] + [along_before(1), along_before(-1)]
    peers += [other_core] + [along_x(1), along_x(3)]
    for peer in peers:
        pl.semaphore_signal(barrier, inc=1, device_id=peer, device_id_type=MESH)

    sends = []

    def send(src, dst, send_sem, recv_sem, device):
        copy = pltpu.make_async_remote_copy(
            src_ref=src, dst_ref=dst, send_sem=send_sem, recv_sem=recv_sem,
            device_id=device, device_id_type=MESH,
        )
        copy.start()
        sends.append(copy)
        return copy

    def drain(count):
        for copy in sends[:count]:
            copy.wait_send()
        del sends[:count]

    inputs[0].wait()
    inputs[1].wait()
    size_row = size_ref[...].astype(jnp.float32)
    owner_row = owner_ref[...].astype(jnp.float32)
    n_block = size_row.shape[1]
    rows, cols = iota((n_block, n_block), 0), iota((n_block, n_block), 1)
    zero = jnp.zeros((n_block, n_block), jnp.float32)
    size_col = jnp.sum(jnp.where(rows == cols, size_row + zero, 0.0), axis=1, keepdims=True)
    owner_col = jnp.sum(jnp.where(rows == cols, owner_row + zero, 0.0), axis=1, keepdims=True)
    offset_col = jnp.sum(jnp.where(cols < rows, size_row + zero, 0.0), axis=1, keepdims=True)

    mine = owner_col == pair.astype(jnp.float32)
    my_offset = jnp.sum(jnp.where(mine, offset_col, 0.0), axis=0, keepdims=True).astype(jnp.int32)
    n_msg = 8 * 16
    at = iota((n_msg, CAP), 0)
    slot = iota((n_msg, CAP), 1)
    wanted = jnp.where(
        ((slot + my_offset) & 7) == (at >> 4), (at & 15) - parts * (slot >> 3), -1
    )
    choose = [jnp.where(wanted == q, 1.0, 0.0).astype(jnp.bfloat16) for q in range(parts)]
    inputs[2].wait()
    load = pltpu.make_async_copy(b_hbm, b_ref, b_sem.at[0])
    load.start()
    for a in range(PIECES):
        total = jnp.zeros((n_msg, lane), jnp.float32)
        for q in range(parts):
            start = a * piece + q * lane
            total += jnp.dot(
                choose[q], a_ref[:, start : start + lane], preferred_element_type=jnp.float32
            )
        msg[a] = total.astype(jnp.bfloat16).reshape(8, 16, lane)

    pl.semaphore_wait(barrier, len(peers))

    phase0 = [
        send(
            msg.at[:, lax.rem(me + d, 8)], got.at[:, 0, me], send0.at[d - 1], recv0.at[d - 1], along(d)
        )
        for d in range(1, 8)
    ]
    for a in range(PIECES):
        got[a, 0, me] = msg[a, me]

    width = got.shape[1] * n_msg
    place = iota((1, width), 1)
    slot_of = place >> 7
    source = (place >> 4) & 7
    m = place & 15
    i = jnp.where(m >= parts, 1, 0) + jnp.where(m >= 2 * parts, 1, 0) + jnp.where(m >= 3 * parts, 1, 0)
    q = m - parts * i
    step = (slot_of + 1) >> 1
    ring = jnp.where((slot_of & 1) == 0, step, 8 - step)

    owner = ((ring + me_before) & 7) * (8 - 7 * core) + source * (1 + 7 * core)
    hit = owner_col == owner.astype(jnp.float32)
    first = jnp.sum(jnp.where(hit, offset_col, 0.0), axis=0, keepdims=True).astype(jnp.int32)
    count = jnp.sum(jnp.where(hit, size_col, 0.0), axis=0, keepdims=True).astype(jnp.int32)
    k = ((first - me + 7) >> 3) + i
    good = (8 * k + me < first + count) & (i < 3)
    target = q * 128 + ((k >> 4) & 1) * 64 + (k >> 5) * 16 + (k & 15)
    target = jnp.where(good, target, -1)

    for copy in phase0:
        copy.wait_recv()

    def ring_send(view, n_rows, a, way, step, send_sem, recv_sem, device):
        src = 0 if step == 0 else 2 * step - 1 + way
        dst = 7 if step == 3 else 2 * step + 1 + way
        rows = pl.ds(0, n_rows) if step < 3 else pl.ds(way * (n_rows // 2), n_rows // 2)
        return send(
            view(a, src, rows), view(a, dst, rows),
            send_sem.at[way, step, a], recv_sem.at[way, step, a], device(1 if way == 0 else -1),
        )

    flying1, flying2 = {}, {}

    def first_ring(step, a, way):
        flying1[step, a, way] = ring_send(
            lambda a, slot, rows: got.at[a, slot, rows], 8, a, way, step, send1, recv1, along_before
        )

    def second_ring(step, a, way):
        flying2[step, a, way] = ring_send(
            lambda a, slot, rows: blocks.at[slot, rows, pl.ds(a * piece, piece)], 128,
            a, way, step, send2, recv2, along,
        )

    for a in range(PIECES):
        for way in range(2):
            first_ring(0, a, way)

    def fill(part, carry):
        row = iota((128, width), 0) + part * 128
        sel[pl.ds(part * 128, 128)] = jnp.where(row == target, 1.0, 0.0).astype(jnp.bfloat16)
        return carry

    lax.fori_loop(0, parts, fill, 0)
    for step in range(3):
        for a in range(PIECES):
            for way in range(2):
                flying1[step, a, way].wait_recv()
                first_ring(step + 1, a, way)
        if step == 0:
            acc[...] = jnp.zeros_like(acc)
        if step == 1:
            early[...] = jnp.dot(
                sel[:, : 5 * n_msg], got[0, :5].reshape(5 * n_msg, lane), preferred_element_type=jnp.float32
            )

    n_early = len(sends)

    for a in range(PIECES):
        for way in range(2):
            flying1[3, a, way].wait_recv()
        if a == 0:
            value = early[...] + jnp.dot(
                sel[:, 5 * n_msg :], got[0, 5:].reshape(3 * n_msg, lane), preferred_element_type=jnp.float32
            )
        else:
            value = jnp.dot(sel[...], got[a].reshape(width, lane), preferred_element_type=jnp.float32)
        value = value.astype(jnp.bfloat16)
        for q in range(parts):
            start = a * piece + q * lane
            blocks[0, :, start : start + lane] = value[q * 128 : q * 128 + 128]
        for way in range(2):
            second_ring(0, a, way)

    first_table, second_table, name_table = order_tables()
    where_to = pick(first_table, delta) * (1 - core) + pick(second_table, delta) * core
    names = pick(name_table, delta)

    def multiply(slot0, n_slot, a):
        if a % 2 == 0:
            return
        columns = pl.ds((a - 1) * piece, 2 * piece)
        left = blocks[slot0 : slot0 + n_slot, :, columns].reshape(n_slot * 128, 2 * piece)
        value = lax.dot_general(
            left, b_ref[:, columns], (((1,), (1,)), ((), ())), preferred_element_type=jnp.float32
        )
        for s in range(n_slot):
            pos = digit(where_to, slot0 + s)
            for c in range(2):
                acc[c, pos] += value[s * 128 + c * 64 : s * 128 + c * 64 + 64]

    def arrive(step, a):
        for way in range(2):
            flying2[step, a, way].wait_recv()
            if step < 3:
                second_ring(step + 1, a, way)

    def core_send(g):
        lo, hi = GROUPS[g]
        return send(
            acc.at[1 - core, pl.ds(lo, hi - lo)], from_core.at[pl.ds(lo, hi - lo)],
            send_c.at[g], recv_c.at[g], other_core,
        )

    right, left, opposite = (lax.rem(x + d, NX) for d in (1, 3, 2))

    def x_first(g, exchanged):
        lo, hi = GROUPS[g]
        exchanged.wait_recv()
        for t in range(NX):
            sums[t, lo:hi] = acc[core, lo:hi, t * 16 : t * 16 + 16] + from_core[lo:hi, t * 16 : t * 16 + 16]
        return [
            send(
                sums.at[opposite, pl.ds(lo, hi - lo), pl.ds(w * 8, 8)], from_opposite.at[w, pl.ds(lo, hi - lo)],
                send_o.at[g, w], recv_o.at[g, w], along_x((1, 3)[w]),
            )
            for w in range(2)
        ]

    def x_second(g, copies):
        lo, hi = GROUPS[g]
        out = []
        for w, near in ((0, right), (1, left)):
            copies[w].wait_recv()
            sums[near, lo:hi, w * 8 : w * 8 + 8] += from_opposite[w, lo:hi]
            out.append(
                send(
                    sums.at[near, pl.ds(lo, hi - lo)], from_x.at[w, pl.ds(lo, hi - lo)],
                    send_x.at[g, w], recv_x.at[g, w], along_x((1, 3)[w]),
                )
            )
        return out

    def finish(g, copies):
        lo, hi = GROUPS[g]
        for copy in copies:
            copy.wait_recv()
        value = sums[x, lo:hi] + from_x[0, lo:hi] + from_x[1, lo:hi]
        final[lo:hi] = value.astype(jnp.bfloat16)

    load.wait()
    for a in range(PIECES):
        multiply(0, 1, a)
    for step in range(2):
        for a in range(PIECES):
            arrive(step, a)
            multiply(2 * step + 1, 2, a)
            if step == 0 and a == 1:
                drain(n_early)
    core_a = core_send(0)
    n_early = len(sends)
    for a in range(PIECES):
        arrive(2, a)
        if a == 0:
            x_a = x_first(0, core_a)
        if a == 2:
            x_a = x_second(0, x_a)
        multiply(5, 2, a)
    core_b = core_send(1)
    for a in range(PIECES):
        arrive(3, a)
        if a == 1:
            x_b = x_first(1, core_b)
        multiply(7, 1, a)
        if a == 3:
            x_b = x_second(1, x_b)
            drain(n_early)
            finish(0, x_a)
    core_c = core_send(2)
    row, col = iota((128, 128), 0), iota((128, 128), 1)
    pos = col >> 4
    cls = jnp.zeros((128, 128), jnp.int32)
    for n in range(8):
        cls = jnp.where(pos == n, lax.rem(digit(names, n) + z, 8), cls)
    order = jnp.where(row == (col & 15) * 8 + cls, 1.0, 0.0).astype(jnp.bfloat16)
    x_c = x_second(2, x_first(2, core_c))
    finish(1, x_b)
    drain(len(sends) - 4)
    finish(2, x_c)
    value = jnp.dot(order, final[...].reshape(128, final.shape[-1]), preferred_element_type=jnp.float32)
    out_ref[...] = value.astype(jnp.bfloat16)
    drain(len(sends))


def on_device(amplitudes, integrals, block_size, block_owner):
    slots, depth = amplitudes.shape
    ab = integrals.shape[0]
    lane = depth // PIECES // 5
    n_blocks = block_size.shape[0]
    vmem = pl.BlockSpec(memory_space=pltpu.VMEM)
    dma = pltpu.SemaphoreType.DMA
    return pl.pallas_call(
        kernel,
        out_shape=jax.ShapeDtypeStruct((128, ab), jnp.bfloat16),
        in_specs=[pl.BlockSpec(memory_space=pltpu.HBM)] * 4,
        out_specs=vmem,
        scratch_shapes=[
            pltpu.VMEM((slots, depth), jnp.bfloat16),
            pltpu.VMEM((1, n_blocks), jnp.int32),
            pltpu.VMEM((1, n_blocks), jnp.int32),
            pltpu.VMEM((PIECES, 8, 16, lane), jnp.bfloat16),
            pltpu.VMEM((PIECES, 8, 8, 16, lane), jnp.bfloat16),
            pltpu.VMEM((5 * 128, 8 * 128), jnp.bfloat16),
            pltpu.VMEM((8, 128, depth), jnp.bfloat16),
            pltpu.VMEM((ab, depth), jnp.bfloat16),
            pltpu.VMEM((2, 8, 64, ab), jnp.float32),
            pltpu.VMEM((5 * 128, lane), jnp.float32),
            pltpu.VMEM((8, 64, ab), jnp.float32),
            pltpu.VMEM((NX, 8, 16, ab), jnp.float32),
            pltpu.VMEM((2, 8, 8, ab), jnp.float32),
            pltpu.VMEM((2, 8, 16, ab), jnp.float32),
            pltpu.VMEM((8, 16, ab), jnp.bfloat16),
            dma((3,)),
            dma((1,)),
            dma((7,)),
            dma((7,)),
            dma((2, 4, PIECES)),
            dma((2, 4, PIECES)),
            dma((2, 4, PIECES)),
            dma((2, 4, PIECES)),
            dma((3,)),
            dma((3,)),
            dma((3, 2)),
            dma((3, 2)),
            dma((3, 2)),
            dma((3, 2)),
        ],
        compiler_params=pltpu.CompilerParams(
            collective_id=0, has_side_effects=True, vmem_limit_bytes=60 * 1024 * 1024
        ),
        cost_estimate=pl.CostEstimate(
            flops=2 * 1024 * ab * depth, bytes_accessed=2 * ab * depth, transcendentals=0
        ),
    )(
        amplitudes,
        integrals,
        block_size.reshape(1, n_blocks),
        block_owner.reshape(1, n_blocks),
    )


def solution(mesh):
    in_specs = (P("pair", "ctr"), P("pair", "ctr"), P(), P())
    return jax.shard_map(
        on_device, mesh=mesh, in_specs=in_specs, out_specs=P("ctr", "pair"), check_vma=False
    )
```

```python
import functools

import jax
import jax.numpy as jnp
import numpy as np
from jax import lax
from jax.experimental import pallas as pl
from jax.experimental.pallas import tpu as pltpu
from jax.sharding import PartitionSpec as P

MESH = pl.DeviceIdType.MESH
NY = 8
NZ = 8
NX = 4
CAP = 24
PIECES = 3
OFFS = (0, -1, 1, -2, 2, -3, 3, -4)
GROUPS = ((0, 2), (2, 6), (6, 8))


def ring_distance(d):
    d = d % 8
    return min(d, 8 - d)


def order_tables():
    first, second, names = [], [], []
    for delta in range(8):
        order = sorted(range(8), key=lambda o: (max(ring_distance(o), ring_distance(o - delta)), o))
        done = [max(ring_distance(o), ring_distance(o - delta)) for o in order]
        assert done[1] <= 2 and done[5] <= 3
        first.append(sum(order.index(OFFS[s] % 8) * 8**s for s in range(8)))
        second.append(sum(order.index((delta + OFFS[s]) % 8) * 8**s for s in range(8)))
        names.append(sum(order[i] * 8**i for i in range(8)))
    return first, second, names


def pick(table, delta):
    total = 0
    for d in range(8):
        total = total + table[d] * (1 - lax.div(lax.rem(delta - d + 8, 8) + 7, 8))
    return total


def digit(packed, i):
    return lax.rem(lax.div(packed, 8**i), 8)


def iota(shape, dim):
    return lax.broadcasted_iota(jnp.int32, shape, dim)


def kernel(
    a_hbm, b_hbm, table_ref, out_ref,
    a_ref, msg, got, sel, blocks, b_ref, acc, early, from_core, sums, from_opposite, from_x, final,
    in_sem, b_sem, send0, recv0, send1, recv1, send2, recv2, send_c, recv_c, send_o, recv_o, send_x, recv_x,
):
    pair = lax.axis_index("pair")
    ctr = lax.axis_index("ctr")
    y, z = lax.div(pair, NZ), lax.rem(pair, NZ)
    x, core = lax.div(ctr, 2), lax.rem(ctr, 2)
    delta = lax.rem(y - z + 8, 8)
    half = a_ref.shape[1] // 2
    lane = got.shape[-1]
    piece = half // PIECES
    parts = piece // lane

    def along(axis, d):
        if axis == "y":
            return (lax.rem(y + d + NY, NY) * NZ + z, ctr)
        return (y * NZ + lax.rem(z + d + NZ, NZ), ctr)

    other_core = (pair, ctr + 1 - 2 * core)

    def along_x(d):
        return (pair, lax.rem(x + d, NX) * 2 + core)

    load_a = pltpu.make_async_copy(a_hbm, a_ref, in_sem.at[0])
    load_a.start()

    barrier = pltpu.get_barrier_semaphore()
    peers = [along("y", d) for d in range(1, 8)] + [along("z", d) for d in range(1, 8)]
    peers += [other_core] + [along_x(1), along_x(3)]
    for peer in peers:
        pl.semaphore_signal(barrier, inc=1, device_id=peer, device_id_type=MESH)

    sends = []

    def send(src, dst, send_sem, recv_sem, device):
        copy = pltpu.make_async_remote_copy(
            src_ref=src, dst_ref=dst, send_sem=send_sem, recv_sem=recv_sem,
            device_id=device, device_id_type=MESH,
        )
        copy.start()
        sends.append(copy)
        return copy

    def drain(count):
        for copy in sends[:count]:
            copy.wait_send()
        del sends[:count]

    size_row = (table_ref[...] >> 6).astype(jnp.float32)
    owner_row = (table_ref[...] & 63).astype(jnp.float32)
    n_block = size_row.shape[1]
    rows, cols = iota((n_block, n_block), 0), iota((n_block, n_block), 1)
    zero = jnp.zeros((n_block, n_block), jnp.float32)
    size_col = jnp.sum(jnp.where(rows == cols, size_row + zero, 0.0), axis=1, keepdims=True)
    owner_col = jnp.sum(jnp.where(rows == cols, owner_row + zero, 0.0), axis=1, keepdims=True)
    offset_col = jnp.sum(jnp.where(cols < rows, size_row + zero, 0.0), axis=1, keepdims=True)

    mine = owner_col == pair.astype(jnp.float32)
    my_offset = jnp.sum(jnp.where(mine, offset_col, 0.0), axis=0, keepdims=True).astype(jnp.int32)
    n_msg = 8 * 16
    at = iota((n_msg, CAP), 0)
    slot = iota((n_msg, CAP), 1)
    wanted = jnp.where(
        ((slot + my_offset) & 7) == (at >> 4), (at & 15) - parts * (slot >> 3), -1
    )
    choose = [jnp.where(wanted == q, 1.0, 0.0).astype(jnp.bfloat16) for q in range(parts)]
    load_a.wait()
    loads = []
    for h in range(2):
        load = pltpu.make_async_copy(b_hbm.at[:, pl.ds(h * half, half)], b_ref.at[h], b_sem.at[h])
        load.start()
        loads.append(load)

    for h in range(2):
        for a in range(PIECES):
            total = jnp.zeros((n_msg, lane), jnp.float32)
            for q in range(parts):
                start = h * half + a * piece + q * lane
                total += jnp.dot(
                    choose[q], a_ref[:, start : start + lane], preferred_element_type=jnp.float32
                )
            msg[h, a] = total.astype(jnp.bfloat16).reshape(8, 16, lane)

    pl.semaphore_wait(barrier, len(peers))

    phase0 = []
    for d in range(1, 8):
        for h, axis, me in ((0, "z", z), (1, "y", y)):
            phase0.append(
                send(
                    msg.at[h, :, lax.rem(me + d, 8)], got.at[h, :, 0, me],
                    send0.at[h, d - 1], recv0.at[h, d - 1], along(axis, d),
                )
            )
    for a in range(PIECES):
        got[0, a, 0, z] = msg[0, a, z]
        got[1, a, 0, y] = msg[1, a, y]

    width = got.shape[2] * n_msg
    place = iota((1, width), 1)
    slot_of = place >> 7
    source = (place >> 4) & 7
    m = place & 15
    i = jnp.where(m >= parts, 1, 0) + jnp.where(m >= 2 * parts, 1, 0) + jnp.where(m >= 3 * parts, 1, 0)
    q = m - parts * i
    step = (slot_of + 1) >> 1
    ring = jnp.where((slot_of & 1) == 0, step, 8 - step)

    targets = []
    for h in range(2):
        if h == 0:
            owner = ((ring + y) & 7) * NZ + source
            cls = z
        else:
            owner = source * NZ + ((ring + z) & 7)
            cls = y
        hit = owner_col == owner.astype(jnp.float32)
        first = jnp.sum(jnp.where(hit, offset_col, 0.0), axis=0, keepdims=True).astype(jnp.int32)
        count = jnp.sum(jnp.where(hit, size_col, 0.0), axis=0, keepdims=True).astype(jnp.int32)
        k = ((first - cls + 7) >> 3) + i
        good = (8 * k + cls < first + count) & (i < 3)
        target = q * 128 + ((k >> 4) & 1) * 64 + (k >> 5) * 16 + (k & 15)
        targets.append(jnp.where(good, target, -1))

    def select(h):
        def fill(part, carry):
            row = iota((128, width), 0) + part * 128
            sel[h, pl.ds(part * 128, 128)] = jnp.where(row == targets[h], 1.0, 0.0).astype(jnp.bfloat16)
            return carry

        lax.fori_loop(0, parts, fill, 0)

    for copy in phase0:
        copy.wait_recv()

    lanes = (("y", "z"), ("z", "y"))

    def ring_send(view, n_rows, h, a, way, step, send_sem, recv_sem, axis):
        src = 0 if step == 0 else 2 * step - 1 + way
        dst = 7 if step == 3 else 2 * step + 1 + way
        rows = pl.ds(0, n_rows) if step < 3 else pl.ds(way * (n_rows // 2), n_rows // 2)
        return send(
            view(h, a, src, rows), view(h, a, dst, rows),
            send_sem.at[h, way, step, a], recv_sem.at[h, way, step, a],
            along(axis, 1 if way == 0 else -1),
        )

    flying1, flying2 = {}, {}

    def first_ring(step, a, h, way):
        flying1[step, a, h, way] = ring_send(
            lambda h, a, slot, rows: got.at[h, a, slot, rows], 8,
            h, a, way, step, send1, recv1, lanes[h][0],
        )

    def second_ring(step, a, h, way):
        flying2[step, a, h, way] = ring_send(
            lambda h, a, slot, rows: blocks.at[h, slot, rows, pl.ds(a * piece, piece)], 128,
            h, a, way, step, send2, recv2, lanes[h][1],
        )

    both = [(h, way) for way in range(2) for h in range(2)]
    for a in range(PIECES):
        for h, way in both:
            first_ring(0, a, h, way)
    select(0)
    acc[...] = jnp.zeros_like(acc)
    for step in range(3):
        for a in range(PIECES):
            for h, way in both:
                flying1[step, a, h, way].wait_recv()
                first_ring(step + 1, a, h, way)
        if step == 0:
            select(1)
        if step == 1:
            for h in range(2):
                early[h] = jnp.dot(
                    sel[h, :, : 5 * n_msg], got[h, 0, :5].reshape(5 * n_msg, lane),
                    preferred_element_type=jnp.float32,
                )

    n_early = len(sends)

    for a in range(PIECES):
        for h in range(2):
            for way in range(2):
                flying1[3, a, h, way].wait_recv()
            if a == 0:
                value = early[h] + jnp.dot(
                    sel[h, :, 5 * n_msg :], got[h, 0, 5:].reshape(3 * n_msg, lane),
                    preferred_element_type=jnp.float32,
                )
            else:
                value = jnp.dot(
                    sel[h], got[h, a].reshape(width, lane), preferred_element_type=jnp.float32
                )
            value = value.astype(jnp.bfloat16)
            for q in range(parts):
                start = a * piece + q * lane
                blocks[h, 0, :, start : start + lane] = value[q * 128 : q * 128 + 128]
            for way in range(2):
                second_ring(0, a, h, way)

    first_table, second_table, name_table = order_tables()
    where_to = (pick(first_table, delta), pick(second_table, delta))
    names = pick(name_table, delta)

    def multiply(slot0, n_slot, a):
        for h in range(2):
            columns = pl.ds(a * piece, piece)
            left = blocks[h, slot0 : slot0 + n_slot, :, columns].reshape(n_slot * 128, piece)
            value = lax.dot_general(
                left, b_ref[h, :, columns], (((1,), (1,)), ((), ())), preferred_element_type=jnp.float32
            )
            for s in range(n_slot):
                pos = digit(where_to[h], slot0 + s)
                for c in range(2):
                    acc[c, pos] += value[s * 128 + c * 64 : s * 128 + c * 64 + 64]

    def arrive(step, a):
        for h, way in both:
            flying2[step, a, h, way].wait_recv()
            if step < 3:
                second_ring(step + 1, a, h, way)

    def core_send(g):
        lo, hi = GROUPS[g]
        return send(
            acc.at[1 - core, pl.ds(lo, hi - lo)], from_core.at[pl.ds(lo, hi - lo)],
            send_c.at[g], recv_c.at[g], other_core,
        )

    right, left, opposite = (lax.rem(x + d, NX) for d in (1, 3, 2))

    def x_first(g, exchanged):
        lo, hi = GROUPS[g]
        exchanged.wait_recv()
        for t in range(NX):
            sums[t, lo:hi] = acc[core, lo:hi, t * 16 : t * 16 + 16] + from_core[lo:hi, t * 16 : t * 16 + 16]
        return [
            send(
                sums.at[opposite, pl.ds(lo, hi - lo), pl.ds(w * 8, 8)], from_opposite.at[w, pl.ds(lo, hi - lo)],
                send_o.at[g, w], recv_o.at[g, w], along_x((1, 3)[w]),
            )
            for w in range(2)
        ]

    def x_second(g, copies):
        lo, hi = GROUPS[g]
        out = []
        for w, near in ((0, right), (1, left)):
            copies[w].wait_recv()
            sums[near, lo:hi, w * 8 : w * 8 + 8] += from_opposite[w, lo:hi]
            out.append(
                send(
                    sums.at[near, pl.ds(lo, hi - lo)], from_x.at[w, pl.ds(lo, hi - lo)],
                    send_x.at[g, w], recv_x.at[g, w], along_x((1, 3)[w]),
                )
            )
        return out

    def finish(g, copies):
        lo, hi = GROUPS[g]
        for copy in copies:
            copy.wait_recv()
        value = sums[x, lo:hi] + from_x[0, lo:hi] + from_x[1, lo:hi]
        final[lo:hi] = value.astype(jnp.bfloat16)

    for load in loads:
        load.wait()
    for a in range(PIECES):
        multiply(0, 1, a)
    for step in range(2):
        for a in range(PIECES):
            arrive(step, a)
            multiply(2 * step + 1, 2, a)
            if step == 0 and a == 0:
                drain(n_early)
    core_a = core_send(0)
    n_early = len(sends)
    for a in range(PIECES):
        arrive(2, a)
        if a == 0:
            x_a = x_first(0, core_a)
        if a == 1:
            x_a = x_second(0, x_a)
        multiply(5, 2, a)
    core_b = core_send(1)
    for a in range(PIECES):
        arrive(3, a)
        if a == 0:
            x_b = x_first(1, core_b)
        multiply(7, 1, a)
        if a == 1:
            x_b = x_second(1, x_b)
            drain(n_early)
            finish(0, x_a)
    core_c = core_send(2)
    row, col = iota((128, 128), 0), iota((128, 128), 1)
    pos = col >> 4
    cls = jnp.zeros((128, 128), jnp.int32)
    for n in range(8):
        cls = jnp.where(pos == n, lax.rem(digit(names, n) + z, 8), cls)
    order = jnp.where(row == (col & 15) * 8 + cls, 1.0, 0.0).astype(jnp.bfloat16)
    x_c = x_second(2, x_first(2, core_c))
    finish(1, x_b)
    drain(len(sends) - 4)
    finish(2, x_c)
    value = jnp.dot(order, final[...].reshape(128, final.shape[-1]), preferred_element_type=jnp.float32)
    out_ref[...] = value.astype(jnp.bfloat16)
    drain(len(sends))


def on_device(amplitudes, integrals, block_size, block_owner):
    slots, depth = amplitudes.shape
    ab = integrals.shape[0]
    half = depth // 2
    lane = half // PIECES // 5
    n_blocks = block_size.shape[0]
    vmem = pl.BlockSpec(memory_space=pltpu.VMEM)
    dma = pltpu.SemaphoreType.DMA
    return pl.pallas_call(
        kernel,
        out_shape=jax.ShapeDtypeStruct((128, ab), jnp.bfloat16),
        in_specs=[pl.BlockSpec(memory_space=pltpu.HBM)] * 2 + [vmem],
        out_specs=vmem,
        scratch_shapes=[
            pltpu.VMEM((slots, depth), jnp.bfloat16),
            pltpu.VMEM((2, PIECES, 8, 16, lane), jnp.bfloat16),
            pltpu.VMEM((2, PIECES, 8, 8, 16, lane), jnp.bfloat16),
            pltpu.VMEM((2, 5 * 128, 8 * 128), jnp.bfloat16),
            pltpu.VMEM((2, 8, 128, half), jnp.bfloat16),
            pltpu.VMEM((2, ab, half), jnp.bfloat16),
            pltpu.VMEM((2, 8, 64, ab), jnp.float32),
            pltpu.VMEM((2, 5 * 128, lane), jnp.float32),
            pltpu.VMEM((8, 64, ab), jnp.float32),
            pltpu.VMEM((NX, 8, 16, ab), jnp.float32),
            pltpu.VMEM((2, 8, 8, ab), jnp.float32),
            pltpu.VMEM((2, 8, 16, ab), jnp.float32),
            pltpu.VMEM((8, 16, ab), jnp.bfloat16),
            dma((1,)),
            dma((2,)),
            dma((2, 7)),
            dma((2, 7)),
            dma((2, 2, 4, PIECES)),
            dma((2, 2, 4, PIECES)),
            dma((2, 2, 4, PIECES)),
            dma((2, 2, 4, PIECES)),
            dma((3,)),
            dma((3,)),
            dma((3, 2)),
            dma((3, 2)),
            dma((3, 2)),
            dma((3, 2)),
        ],
        compiler_params=pltpu.CompilerParams(
            collective_id=0, has_side_effects=True, vmem_limit_bytes=55040 * 1024
        ),
        cost_estimate=pl.CostEstimate(
            flops=2 * 1024 * ab * depth, bytes_accessed=2 * ab * depth, transcendentals=0
        ),
    )(
        amplitudes,
        integrals,
        (block_size * 64 + block_owner).reshape(1, n_blocks),
    )


def solution(mesh):
    in_specs = (P("pair", "ctr"), P("pair", "ctr"), P(), P())
    return jax.shard_map(
        on_device, mesh=mesh, in_specs=in_specs, out_specs=P("ctr", "pair"), check_vma=False
    )
```

```python
import functools

import jax
import jax.numpy as jnp
import numpy as np
from jax import lax
from jax.experimental import pallas as pl
from jax.experimental.pallas import tpu as pltpu
from jax.sharding import PartitionSpec as P

MESH = pl.DeviceIdType.MESH
NY = 8
NZ = 8
NX = 4
CAP = 24
PIECES = 3
OFFS = (0, -1, 1, -2, 2, -3, 3, -4)
GROUPS = ((0, 2, 0, 64), (2, 6, 0, 64), (6, 8, 0, 32), (6, 8, 32, 64))


def ring_distance(d):
    d = d % 8
    return min(d, 8 - d)


def order_tables():
    first, second, names = [], [], []
    for delta in range(8):
        order = sorted(range(8), key=lambda o: (max(ring_distance(o), ring_distance(o - delta)), o))
        done = [max(ring_distance(o), ring_distance(o - delta)) for o in order]
        assert done[1] <= 2 and done[5] <= 3
        first.append(sum(order.index(OFFS[s] % 8) * 8**s for s in range(8)))
        second.append(sum(order.index((delta + OFFS[s]) % 8) * 8**s for s in range(8)))
        names.append(sum(order[i] * 8**i for i in range(8)))
    return first, second, names


def pick(table, delta):
    total = 0
    for d in range(8):
        total = total + table[d] * (1 - lax.div(lax.rem(delta - d + 8, 8) + 7, 8))
    return total


def digit(packed, i):
    return lax.rem(lax.div(packed, 8**i), 8)


def iota(shape, dim):
    return lax.broadcasted_iota(jnp.int32, shape, dim)


def kernel(
    a_hbm, b_hbm, table_ref, out_ref,
    a_ref, msg, got, sel, blocks, b_ref, acc, early, from_core, sums, from_opposite, from_x, final,
    in_sem, b_sem, send0, recv0, send1, recv1, send2, recv2, send_c, recv_c, send_o, recv_o, send_x, recv_x,
):
    pair = lax.axis_index("pair")
    ctr = lax.axis_index("ctr")
    y, z = lax.div(pair, NZ), lax.rem(pair, NZ)
    x, core = lax.div(ctr, 2), lax.rem(ctr, 2)
    delta = lax.rem(y - z + 8, 8)
    half = a_ref.shape[1] // 2
    lane = got.shape[-1]
    piece = half // PIECES
    parts = piece // lane

    def along(axis, d):
        if axis == "y":
            return (lax.rem(y + d + NY, NY) * NZ + z, ctr)
        return (y * NZ + lax.rem(z + d + NZ, NZ), ctr)

    other_core = (pair, ctr + 1 - 2 * core)

    def along_x(d):
        return (pair, lax.rem(x + d, NX) * 2 + core)

    load_a = pltpu.make_async_copy(a_hbm, a_ref, in_sem.at[0])
    load_a.start()

    barrier = pltpu.get_barrier_semaphore()
    peers = [along("y", d) for d in range(1, 8)] + [along("z", d) for d in range(1, 8)]
    peers += [other_core] + [along_x(1), along_x(3)]
    for peer in peers:
        pl.semaphore_signal(barrier, inc=1, device_id=peer, device_id_type=MESH)

    sends = []

    def send(src, dst, send_sem, recv_sem, device):
        copy = pltpu.make_async_remote_copy(
            src_ref=src, dst_ref=dst, send_sem=send_sem, recv_sem=recv_sem,
            device_id=device, device_id_type=MESH,
        )
        copy.start()
        sends.append(copy)
        return copy

    def drain(count):
        for copy in sends[:count]:
            copy.wait_send()
        del sends[:count]

    size_row = (table_ref[...] >> 6).astype(jnp.float32)
    owner_row = (table_ref[...] & 63).astype(jnp.float32)
    n_block = size_row.shape[1]
    rows, cols = iota((n_block, n_block), 0), iota((n_block, n_block), 1)
    zero = jnp.zeros((n_block, n_block), jnp.float32)
    size_col = jnp.sum(jnp.where(rows == cols, size_row + zero, 0.0), axis=1, keepdims=True)
    owner_col = jnp.sum(jnp.where(rows == cols, owner_row + zero, 0.0), axis=1, keepdims=True)
    offset_col = jnp.sum(jnp.where(cols < rows, size_row + zero, 0.0), axis=1, keepdims=True)

    mine = owner_col == pair.astype(jnp.float32)
    my_offset = jnp.sum(jnp.where(mine, offset_col, 0.0), axis=0, keepdims=True).astype(jnp.int32)
    n_msg = 8 * 16
    at = iota((n_msg, CAP), 0)
    slot = iota((n_msg, CAP), 1)
    wanted = jnp.where(
        ((slot + my_offset) & 7) == (at >> 4), (at & 15) - parts * (slot >> 3), -1
    )
    choose = [jnp.where(wanted == q, 1.0, 0.0).astype(jnp.bfloat16) for q in range(parts)]
    load_a.wait()
    loads = []
    for h in range(2):
        load = pltpu.make_async_copy(b_hbm.at[:, pl.ds(h * half, half)], b_ref.at[h], b_sem.at[h])
        load.start()
        loads.append(load)

    for h in range(2):
        for a in range(PIECES):
            total = jnp.zeros((n_msg, lane), jnp.float32)
            for q in range(parts):
                start = h * half + a * piece + q * lane
                total += jnp.dot(
                    choose[q], a_ref[:, start : start + lane], preferred_element_type=jnp.float32
                )
            msg[h, a] = total.astype(jnp.bfloat16).reshape(8, 16, lane)

    pl.semaphore_wait(barrier, len(peers))

    phase0 = []
    for d in range(1, 8):
        for h, axis, me in ((0, "z", z), (1, "y", y)):
            phase0.append(
                send(
                    msg.at[h, :, lax.rem(me + d, 8)], got.at[h, :, 0, me],
                    send0.at[h, d - 1], recv0.at[h, d - 1], along(axis, d),
                )
            )
    for a in range(PIECES):
        got[0, a, 0, z] = msg[0, a, z]
        got[1, a, 0, y] = msg[1, a, y]

    width = got.shape[2] * n_msg
    place = iota((1, width), 1)
    slot_of = place >> 7
    source = (place >> 4) & 7
    m = place & 15
    i = jnp.where(m >= parts, 1, 0) + jnp.where(m >= 2 * parts, 1, 0) + jnp.where(m >= 3 * parts, 1, 0)
    q = m - parts * i
    step = (slot_of + 1) >> 1
    ring = jnp.where((slot_of & 1) == 0, step, 8 - step)

    targets = []
    for h in range(2):
        if h == 0:
            owner = ((ring + y) & 7) * NZ + source
            cls = z
        else:
            owner = source * NZ + ((ring + z) & 7)
            cls = y
        hit = owner_col == owner.astype(jnp.float32)
        first = jnp.sum(jnp.where(hit, offset_col, 0.0), axis=0, keepdims=True).astype(jnp.int32)
        count = jnp.sum(jnp.where(hit, size_col, 0.0), axis=0, keepdims=True).astype(jnp.int32)
        k = ((first - cls + 7) >> 3) + i
        good = (8 * k + cls < first + count) & (i < 3)
        target = q * 128 + ((k >> 4) & 1) * 64 + ((k >> 3) & 1) * 32 + (k >> 5) * 8 + (k & 7)
        targets.append(jnp.where(good, target, -1))

    def select(h):
        def fill(part, carry):
            row = iota((128, width), 0) + part * 128
            sel[h, pl.ds(part * 128, 128)] = jnp.where(row == targets[h], 1.0, 0.0).astype(jnp.bfloat16)
            return carry

        lax.fori_loop(0, parts, fill, 0)

    for copy in phase0:
        copy.wait_recv()

    lanes = (("y", "z"), ("z", "y"))

    def ring_send(view, n_rows, h, a, way, step, send_sem, recv_sem, axis):
        src = 0 if step == 0 else 2 * step - 1 + way
        dst = 7 if step == 3 else 2 * step + 1 + way
        rows = pl.ds(0, n_rows) if step < 3 else pl.ds(way * (n_rows // 2), n_rows // 2)
        return send(
            view(h, a, src, rows), view(h, a, dst, rows),
            send_sem.at[h, way, step, a], recv_sem.at[h, way, step, a],
            along(axis, 1 if way == 0 else -1),
        )

    flying1, flying2 = {}, {}

    def first_ring(step, a, h, way):
        flying1[step, a, h, way] = ring_send(
            lambda h, a, slot, rows: got.at[h, a, slot, rows], 8,
            h, a, way, step, send1, recv1, lanes[h][0],
        )

    def second_ring(step, a, h, way):
        if step < 3 or a == 0:
            flying2[step, a, h, way] = ring_send(
                lambda h, a, slot, rows: blocks.at[h, slot, rows, pl.ds(a * piece, piece)], 128,
                h, a, way, step, send2, recv2, lanes[h][1],
            )
            return
        rows, columns = pl.ds(way * 64 + (a - 1) * 32, 32), pl.ds(piece, half - piece)
        flying2[step, a, h, way] = send(
            blocks.at[h, 5 + way, rows, columns], blocks.at[h, 7, rows, columns],
            send2.at[h, way, step, a], recv2.at[h, way, step, a],
            along(lanes[h][1], 1 if way == 0 else -1),
        )

    both = [(h, way) for way in range(2) for h in range(2)]
    for a in range(PIECES):
        for h, way in both:
            first_ring(0, a, h, way)
    select(0)
    acc[...] = jnp.zeros_like(acc)
    for step in range(3):
        for a in range(PIECES):
            for h, way in both:
                flying1[step, a, h, way].wait_recv()
                first_ring(step + 1, a, h, way)
        if step == 0:
            select(1)
        if step == 1:
            for h in range(2):
                early[h] = jnp.dot(
                    sel[h, :, : 5 * n_msg], got[h, 0, :5].reshape(5 * n_msg, lane),
                    preferred_element_type=jnp.float32,
                )

    n_early = len(sends)

    for a in range(PIECES):
        for h in range(2):
            for way in range(2):
                flying1[3, a, h, way].wait_recv()
            if a == 0:
                value = early[h] + jnp.dot(
                    sel[h, :, 5 * n_msg :], got[h, 0, 5:].reshape(3 * n_msg, lane),
                    preferred_element_type=jnp.float32,
                )
            else:
                value = jnp.dot(
                    sel[h], got[h, a].reshape(width, lane), preferred_element_type=jnp.float32
                )
            value = value.astype(jnp.bfloat16)
            for q in range(parts):
                start = a * piece + q * lane
                blocks[h, 0, :, start : start + lane] = value[q * 128 : q * 128 + 128]
            for way in range(2):
                second_ring(0, a, h, way)

    first_table, second_table, name_table = order_tables()
    where_to = (pick(first_table, delta), pick(second_table, delta))
    names = pick(name_table, delta)

    def multiply(slot0, n_slot, a):
        for h in range(2):
            columns = pl.ds(a * piece, piece)
            left = blocks[h, slot0 : slot0 + n_slot, :, columns].reshape(n_slot * 128, piece)
            value = lax.dot_general(
                left, b_ref[h, :, columns], (((1,), (1,)), ((), ())), preferred_element_type=jnp.float32
            )
            for s in range(n_slot):
                pos = digit(where_to[h], slot0 + s)
                for c in range(2):
                    acc[c, pos] += value[s * 128 + c * 64 : s * 128 + c * 64 + 64]

    def multiply_rows(r):
        for h in range(2):
            columns = pl.ds(piece, half - piece)
            left = jnp.concatenate(
                [blocks[h, 7, c * 64 + r * 32 : c * 64 + r * 32 + 32, columns] for c in range(2)], axis=0
            )
            value = lax.dot_general(
                left, b_ref[h, :, columns], (((1,), (1,)), ((), ())), preferred_element_type=jnp.float32
            )
            pos = digit(where_to[h], 7)
            for c in range(2):
                acc[c, pos, r * 32 : r * 32 + 32] += value[c * 32 : c * 32 + 32]

    def arrive(step, a):
        for h, way in both:
            flying2[step, a, h, way].wait_recv()
            if step < 2 or (step == 2 and a == 0):
                second_ring(step + 1, a, h, way)
            elif step == 2 and a == 2:
                second_ring(3, 1, h, way)
        if step == 2 and a == 2:
            for h, way in both:
                second_ring(3, 2, h, way)

    def core_send(g):
        lo, hi, row, end = GROUPS[g]
        at = (pl.ds(lo, hi - lo), pl.ds(row, end - row))
        return send(
            acc.at[(1 - core, *at)], from_core.at[at],
            send_c.at[g], recv_c.at[g], other_core,
        )

    width_x = from_opposite.shape[-1]
    right, left, opposite = (lax.rem(x + d, NX) for d in (1, 3, 2))

    def x_first(g, exchanged):
        lo, hi, row, end = GROUPS[g]
        exchanged.wait_recv()
        for t in range(NX):
            for c in range(row // 32, end // 32):
                at = c * 32 + t * 8
                sums[t, lo:hi, c * 8 : c * 8 + 8] = acc[core, lo:hi, at : at + 8] + from_core[lo:hi, at : at + 8]
        at = (pl.ds(lo, hi - lo), pl.ds(row // 4, (end - row) // 4))
        return [
            send(
                sums.at[(opposite, *at, pl.ds(w * width_x, width_x))], from_opposite.at[(w, *at)],
                send_o.at[g, w], recv_o.at[g, w], along_x((1, 3)[w]),
            )
            for w in range(2)
        ]

    def x_second(g, copies):
        lo, hi, row, end = GROUPS[g]
        k0, k1 = row // 4, end // 4
        at = (pl.ds(lo, hi - lo), pl.ds(k0, k1 - k0))
        out = []
        for w, near in ((0, right), (1, left)):
            copies[w].wait_recv()
            sums[near, lo:hi, k0:k1, w * width_x : w * width_x + width_x] += from_opposite[w, lo:hi, k0:k1]
            out.append(
                send(
                    sums.at[(near, *at)], from_x.at[(w, *at)],
                    send_x.at[g, w], recv_x.at[g, w], along_x((1, 3)[w]),
                )
            )
        return out

    def finish(g, copies):
        lo, hi, row, end = GROUPS[g]
        k0, k1 = row // 4, end // 4
        for copy in copies:
            copy.wait_recv()
        final[lo:hi, k0:k1] = sums[x, lo:hi, k0:k1] + from_x[0, lo:hi, k0:k1] + from_x[1, lo:hi, k0:k1]

    for load in loads:
        load.wait()
    for a in range(PIECES):
        multiply(0, 1, a)
    for step in range(2):
        for a in range(PIECES):
            arrive(step, a)
            multiply(2 * step + 1, 2, a)
            if step == 0 and a == 0:
                drain(n_early)
    core_a = core_send(0)
    n_early = len(sends)
    for a in range(PIECES):
        arrive(2, a)
        if a == 0:
            x_a = x_first(0, core_a)
        if a == 1:
            x_a = x_second(0, x_a)
        multiply(5, 2, a)
    core_b = core_send(1)
    arrive(3, 0)
    x_b = x_first(1, core_b)
    multiply(7, 1, 0)
    finish(0, x_a)
    drain(n_early)
    arrive(3, 1)
    multiply_rows(0)
    core_c = core_send(2)
    x_b = x_second(1, x_b)
    row, col = iota((128, 128), 0), iota((128, 128), 1)
    pos = col >> 4
    cls = jnp.zeros((128, 128), jnp.int32)
    for n in range(8):
        cls = jnp.where(pos == n, lax.rem(digit(names, n) + z, 8), cls)
    order = jnp.where(row == (col & 15) * 8 + cls, 1.0, 0.0).astype(jnp.bfloat16)
    x_c = x_first(2, core_c)
    arrive(3, 2)
    multiply_rows(1)
    core_d = core_send(3)
    x_c = x_second(2, x_c)
    x_d = x_first(3, core_d)
    n_early = len(sends) - 7
    finish(1, x_b)
    x_d = x_second(3, x_d)
    drain(n_early)
    finish(2, x_c)
    finish(3, x_d)
    value = jnp.dot(order, final[...].reshape(128, final.shape[-1]).astype(jnp.bfloat16), preferred_element_type=jnp.float32)
    out_ref[...] = value.astype(jnp.bfloat16)
    drain(len(sends))


def on_device(amplitudes, integrals, block_size, block_owner):
    slots, depth = amplitudes.shape
    ab = integrals.shape[0]
    half = depth // 2
    lane = half // PIECES // 5
    n_blocks = block_size.shape[0]
    vmem = pl.BlockSpec(memory_space=pltpu.VMEM)
    dma = pltpu.SemaphoreType.DMA
    return pl.pallas_call(
        kernel,
        out_shape=jax.ShapeDtypeStruct((128, ab), jnp.bfloat16),
        in_specs=[pl.BlockSpec(memory_space=pltpu.HBM)] * 2 + [vmem],
        out_specs=vmem,
        scratch_shapes=[
            pltpu.VMEM((slots, depth), jnp.bfloat16),
            pltpu.VMEM((2, PIECES, 8, 16, lane), jnp.bfloat16),
            pltpu.VMEM((2, PIECES, 8, 8, 16, lane), jnp.bfloat16),
            pltpu.VMEM((2, 5 * 128, 8 * 128), jnp.bfloat16),
            pltpu.VMEM((2, 8, 128, half), jnp.bfloat16),
            pltpu.VMEM((2, ab, half), jnp.bfloat16),
            pltpu.VMEM((2, 8, 64, ab), jnp.float32),
            pltpu.VMEM((2, 5 * 128, lane), jnp.float32),
            pltpu.VMEM((8, 64, ab), jnp.float32),
            pltpu.VMEM((NX, 8, 16, ab), jnp.float32),
            pltpu.VMEM((2, 8, 16, ab // 2), jnp.float32),
            pltpu.VMEM((2, 8, 16, ab), jnp.float32),
            pltpu.VMEM((8, 16, ab), jnp.float32),
            dma((1,)),
            dma((2,)),
            dma((2, 7)),
            dma((2, 7)),
            dma((2, 2, 4, PIECES)),
            dma((2, 2, 4, PIECES)),
            dma((2, 2, 4, PIECES)),
            dma((2, 2, 4, PIECES)),
            dma((4,)),
            dma((4,)),
            dma((4, 2)),
            dma((4, 2)),
            dma((4, 2)),
            dma((4, 2)),
        ],
        compiler_params=pltpu.CompilerParams(
            collective_id=0, has_side_effects=True, vmem_limit_bytes=55040 * 1024
        ),
        cost_estimate=pl.CostEstimate(
            flops=2 * 1024 * ab * depth, bytes_accessed=2 * ab * depth, transcendentals=0
        ),
    )(
        amplitudes,
        integrals,
        (block_size * 64 + block_owner).reshape(1, n_blocks),
    )


def solution(mesh):
    in_specs = (P("pair", "ctr"), P("pair", "ctr"), P(), P())
    return jax.shard_map(
        on_device, mesh=mesh, in_specs=in_specs, out_specs=P("ctr", "pair"), check_vma=False
    )
```

```python
import functools

import jax
import jax.numpy as jnp
import numpy as np
from jax import lax
from jax.experimental import pallas as pl
from jax.experimental.pallas import tpu as pltpu
from jax.sharding import PartitionSpec as P

MESH = pl.DeviceIdType.MESH
NY = 8
NZ = 8
NX = 4
CAP = 24
PIECES = 3
OFFS = (0, -1, 1, -2, 2, -3, 3, -4)
GROUPS = ((0, 2), (2, 6), (6, 8))


def ring_distance(d):
    d = d % 8
    return min(d, 8 - d)


def order_tables():
    first, second, names = [], [], []
    for delta in range(8):
        order = sorted(range(8), key=lambda o: (max(ring_distance(o), ring_distance(o - delta)), o))
        done = [max(ring_distance(o), ring_distance(o - delta)) for o in order]
        assert done[1] <= 2 and done[5] <= 3
        first.append(sum(order.index(OFFS[s] % 8) * 8**s for s in range(8)))
        second.append(sum(order.index((delta + OFFS[s]) % 8) * 8**s for s in range(8)))
        names.append(sum(order[i] * 8**i for i in range(8)))
    return first, second, names


def pick(table, delta):
    total = 0
    for d in range(8):
        total = total + table[d] * (1 - lax.div(lax.rem(delta - d + 8, 8) + 7, 8))
    return total


def digit(packed, i):
    return lax.rem(lax.div(packed, 8**i), 8)


def iota(shape, dim):
    return lax.broadcasted_iota(jnp.int32, shape, dim)


def kernel(
    a_hbm, b_hbm, table_ref, out_ref,
    a_ref, msg, got, sel, blocks, b_ref, acc, early, from_core, sums, from_opposite, from_x, final,
    in_sem, b_sem, send0, recv0, send1, recv1, send2, recv2, send_c, recv_c, send_o, recv_o, send_x, recv_x,
):
    pair = lax.axis_index("pair")
    ctr = lax.axis_index("ctr")
    y, z = lax.div(pair, NZ), lax.rem(pair, NZ)
    x, core = lax.div(ctr, 2), lax.rem(ctr, 2)
    delta = lax.rem(y - z + 8, 8)
    half = a_ref.shape[1] // 2
    lane = got.shape[-1]
    piece = half // PIECES
    parts = piece // lane

    def along(axis, d):
        if axis == "y":
            return (lax.rem(y + d + NY, NY) * NZ + z, ctr)
        return (y * NZ + lax.rem(z + d + NZ, NZ), ctr)

    other_core = (pair, ctr + 1 - 2 * core)

    def along_x(d):
        return (pair, lax.rem(x + d, NX) * 2 + core)

    load_a = pltpu.make_async_copy(a_hbm, a_ref, in_sem.at[0])
    load_a.start()

    barrier = pltpu.get_barrier_semaphore()
    peers = [along("y", d) for d in range(1, 8)] + [along("z", d) for d in range(1, 8)]
    peers += [other_core] + [along_x(1), along_x(3)]
    for peer in peers:
        pl.semaphore_signal(barrier, inc=1, device_id=peer, device_id_type=MESH)

    sends = []

    def send(src, dst, send_sem, recv_sem, device):
        copy = pltpu.make_async_remote_copy(
            src_ref=src, dst_ref=dst, send_sem=send_sem, recv_sem=recv_sem,
            device_id=device, device_id_type=MESH,
        )
        copy.start()
        sends.append(copy)
        return copy

    def drain(count):
        for copy in sends[:count]:
            copy.wait_send()
        del sends[:count]

    size_row = (table_ref[...] >> 6).astype(jnp.float32)
    owner_row = (table_ref[...] & 63).astype(jnp.float32)
    n_block = size_row.shape[1]
    rows, cols = iota((n_block, n_block), 0), iota((n_block, n_block), 1)
    zero = jnp.zeros((n_block, n_block), jnp.float32)
    size_col = jnp.sum(jnp.where(rows == cols, size_row + zero, 0.0), axis=1, keepdims=True)
    owner_col = jnp.sum(jnp.where(rows == cols, owner_row + zero, 0.0), axis=1, keepdims=True)
    offset_col = jnp.sum(jnp.where(cols < rows, size_row + zero, 0.0), axis=1, keepdims=True)

    mine = owner_col == pair.astype(jnp.float32)
    my_offset = jnp.sum(jnp.where(mine, offset_col, 0.0), axis=0, keepdims=True).astype(jnp.int32)
    n_msg = 8 * 16
    at = iota((n_msg, CAP), 0)
    slot = iota((n_msg, CAP), 1)
    wanted = jnp.where(
        ((slot + my_offset) & 7) == (at >> 4), (at & 15) - parts * (slot >> 3), -1
    )
    choose = [jnp.where(wanted == q, 1.0, 0.0).astype(jnp.bfloat16) for q in range(parts)]
    load_a.wait()
    loads = []
    for h in range(2):
        load = pltpu.make_async_copy(b_hbm.at[:, pl.ds(h * half, half)], b_ref.at[h], b_sem.at[h])
        load.start()
        loads.append(load)

    for h in range(2):
        for a in range(PIECES):
            total = jnp.zeros((n_msg, lane), jnp.float32)
            for q in range(parts):
                start = h * half + a * piece + q * lane
                total += jnp.dot(
                    choose[q], a_ref[:, start : start + lane], preferred_element_type=jnp.float32
                )
            msg[h, a] = total.astype(jnp.bfloat16).reshape(8, 16, lane)

    pl.semaphore_wait(barrier, len(peers))

    phase0 = []
    for d in range(1, 8):
        for h, axis, me in ((0, "z", z), (1, "y", y)):
            phase0.append(
                send(
                    msg.at[h, :, lax.rem(me + d, 8)], got.at[h, :, 0, me],
                    send0.at[h, d - 1], recv0.at[h, d - 1], along(axis, d),
                )
            )
    for a in range(PIECES):
        got[0, a, 0, z] = msg[0, a, z]
        got[1, a, 0, y] = msg[1, a, y]

    width = got.shape[2] * n_msg
    place = iota((1, width), 1)
    slot_of = place >> 7
    source = (place >> 4) & 7
    m = place & 15
    i = jnp.where(m >= parts, 1, 0) + jnp.where(m >= 2 * parts, 1, 0) + jnp.where(m >= 3 * parts, 1, 0)
    q = m - parts * i
    step = (slot_of + 1) >> 1
    ring = jnp.where((slot_of & 1) == 0, step, 8 - step)

    targets = []
    for h in range(2):
        if h == 0:
            owner = ((ring + y) & 7) * NZ + source
            cls = z
        else:
            owner = source * NZ + ((ring + z) & 7)
            cls = y
        hit = owner_col == owner.astype(jnp.float32)
        first = jnp.sum(jnp.where(hit, offset_col, 0.0), axis=0, keepdims=True).astype(jnp.int32)
        count = jnp.sum(jnp.where(hit, size_col, 0.0), axis=0, keepdims=True).astype(jnp.int32)
        k = ((first - cls + 7) >> 3) + i
        good = (8 * k + cls < first + count) & (i < 3)
        target = q * 128 + ((k >> 4) & 1) * 64 + (k >> 5) * 16 + (k & 15)
        targets.append(jnp.where(good, target, -1))

    def select(h):
        def fill(part, carry):
            row = iota((128, width), 0) + part * 128
            sel[h, pl.ds(part * 128, 128)] = jnp.where(row == targets[h], 1.0, 0.0).astype(jnp.bfloat16)
            return carry

        lax.fori_loop(0, parts, fill, 0)

    for copy in phase0:
        copy.wait_recv()

    lanes = (("y", "z"), ("z", "y"))

    def ring_send(view, n_rows, h, a, way, step, send_sem, recv_sem, axis):
        src = 0 if step == 0 else 2 * step - 1 + way
        dst = 7 if step == 3 else 2 * step + 1 + way
        rows = pl.ds(0, n_rows) if step < 3 else pl.ds(way * (n_rows // 2), n_rows // 2)
        return send(
            view(h, a, src, rows), view(h, a, dst, rows),
            send_sem.at[h, way, step, a], recv_sem.at[h, way, step, a],
            along(axis, 1 if way == 0 else -1),
        )

    flying1, flying2 = {}, {}

    def first_ring(step, a, h, way):
        flying1[step, a, h, way] = ring_send(
            lambda h, a, slot, rows: got.at[h, a, slot, rows], 8,
            h, a, way, step, send1, recv1, lanes[h][0],
        )

    def second_ring(step, a, h, way):
        flying2[step, a, h, way] = ring_send(
            lambda h, a, slot, rows: blocks.at[h, slot, rows, pl.ds(a * piece, piece)], 128,
            h, a, way, step, send2, recv2, lanes[h][1],
        )

    both = [(h, way) for way in range(2) for h in range(2)]
    for a in range(PIECES):
        for h, way in both:
            first_ring(0, a, h, way)
    select(0)
    acc[...] = jnp.zeros_like(acc)
    for step in range(3):
        for a in range(PIECES):
            for h, way in both:
                flying1[step, a, h, way].wait_recv()
                first_ring(step + 1, a, h, way)
            if step == 2 and a == 0:
                for h in range(2):
                    early[h] += jnp.dot(
                        sel[h, :, 5 * n_msg : 7 * n_msg], got[h, 0, 5:7].reshape(2 * n_msg, lane),
                        preferred_element_type=jnp.float32,
                    )
        if step == 0:
            select(1)
        if step == 1:
            for h in range(2):
                early[h] = jnp.dot(
                    sel[h, :, : 5 * n_msg], got[h, 0, :5].reshape(5 * n_msg, lane),
                    preferred_element_type=jnp.float32,
                )

    n_early = len(sends)

    for a in range(PIECES):
        for h in range(2):
            for way in range(2):
                flying1[3, a, h, way].wait_recv()
            if a == 0:
                value = early[h] + jnp.dot(
                    sel[h, :, 7 * n_msg :], got[h, 0, 7].reshape(n_msg, lane),
                    preferred_element_type=jnp.float32,
                )
            else:
                value = jnp.dot(
                    sel[h], got[h, a].reshape(width, lane), preferred_element_type=jnp.float32
                )
            value = value.astype(jnp.bfloat16)
            for q in range(parts):
                start = a * piece + q * lane
                blocks[h, 0, :, start : start + lane] = value[q * 128 : q * 128 + 128]
            for way in range(2):
                second_ring(0, a, h, way)

    first_table, second_table, name_table = order_tables()
    where_to = (pick(first_table, delta), pick(second_table, delta))
    names = pick(name_table, delta)

    def multiply(slot0, n_slot, a):
        for h in range(2):
            columns = pl.ds(a * piece, piece)
            left = blocks[h, slot0 : slot0 + n_slot, :, columns].reshape(n_slot * 128, piece)
            value = lax.dot_general(
                left, b_ref[h, :, columns], (((1,), (1,)), ((), ())), preferred_element_type=jnp.float32
            )
            for s in range(n_slot):
                pos = digit(where_to[h], slot0 + s)
                for c in range(2):
                    acc[c, pos] += value[s * 128 + c * 64 : s * 128 + c * 64 + 64]

    def arrive(step, a):
        for h, way in both:
            flying2[step, a, h, way].wait_recv()
            if step < 3:
                second_ring(step + 1, a, h, way)

    def core_send(g):
        lo, hi = GROUPS[g]
        return send(
            acc.at[1 - core, pl.ds(lo, hi - lo)], from_core.at[pl.ds(lo, hi - lo)],
            send_c.at[g], recv_c.at[g], other_core,
        )

    right, left, opposite = (lax.rem(x + d, NX) for d in (1, 3, 2))

    def x_first(g, exchanged):
        lo, hi = GROUPS[g]
        exchanged.wait_recv()
        for t in range(NX):
            sums[t, lo:hi] = acc[core, lo:hi, t * 16 : t * 16 + 16] + from_core[lo:hi, t * 16 : t * 16 + 16]
        return [
            send(
                sums.at[opposite, pl.ds(lo, hi - lo), pl.ds(w * 8, 8)], from_opposite.at[w, pl.ds(lo, hi - lo)],
                send_o.at[g, w], recv_o.at[g, w], along_x((1, 3)[w]),
            )
            for w in range(2)
        ]

    def x_second(g, copies):
        lo, hi = GROUPS[g]
        out = []
        for w, near in ((0, right), (1, left)):
            copies[w].wait_recv()
            sums[near, lo:hi, w * 8 : w * 8 + 8] += from_opposite[w, lo:hi]
            out.append(
                send(
                    sums.at[near, pl.ds(lo, hi - lo)], from_x.at[w, pl.ds(lo, hi - lo)],
                    send_x.at[g, w], recv_x.at[g, w], along_x((1, 3)[w]),
                )
            )
        return out

    def finish(g, copies):
        lo, hi = GROUPS[g]
        for copy in copies:
            copy.wait_recv()
        value = sums[x, lo:hi] + from_x[0, lo:hi] + from_x[1, lo:hi]
        final[lo:hi] = value.astype(jnp.bfloat16)

    for load in loads:
        load.wait()
    for a in range(PIECES):
        multiply(0, 1, a)
    for step in range(2):
        for a in range(PIECES):
            arrive(step, a)
            multiply(2 * step + 1, 2, a)
            if step == 0 and a == 0:
                drain(n_early)
    core_a = core_send(0)
    n_early = len(sends)
    for a in range(PIECES):
        arrive(2, a)
        if a == 0:
            x_a = x_first(0, core_a)
        multiply(5, 2, a)
        if a == 1:
            x_a = x_second(0, x_a)
    core_b = core_send(1)
    row, col = iota((128, 128), 0), iota((128, 128), 1)
    pos = col >> 4
    cls = jnp.zeros((128, 128), jnp.int32)
    for n in range(8):
        cls = jnp.where(pos == n, lax.rem(digit(names, n) + z, 8), cls)
    order = jnp.where(row == (col & 15) * 8 + cls, 1.0, 0.0).astype(jnp.bfloat16)
    for a in range(PIECES):
        arrive(3, a)
        if a == 0:
            x_b = x_first(1, core_b)
        multiply(7, 1, a)
        if a == 1:
            x_b = x_second(1, x_b)
            drain(n_early)
            finish(0, x_a)
    core_c = core_send(2)
    x_c = x_second(2, x_first(2, core_c))
    finish(1, x_b)
    drain(len(sends) - 4)
    finish(2, x_c)
    value = jnp.dot(order, final[...].reshape(128, final.shape[-1]), preferred_element_type=jnp.float32)
    out_ref[...] = value.astype(jnp.bfloat16)
    drain(len(sends))


def on_device(amplitudes, integrals, block_size, block_owner):
    slots, depth = amplitudes.shape
    ab = integrals.shape[0]
    half = depth // 2
    lane = half // PIECES // 5
    n_blocks = block_size.shape[0]
    vmem = pl.BlockSpec(memory_space=pltpu.VMEM)
    dma = pltpu.SemaphoreType.DMA
    return pl.pallas_call(
        kernel,
        out_shape=jax.ShapeDtypeStruct((128, ab), jnp.bfloat16),
        in_specs=[pl.BlockSpec(memory_space=pltpu.HBM)] * 2 + [vmem],
        out_specs=vmem,
        scratch_shapes=[
            pltpu.VMEM((slots, depth), jnp.bfloat16),
            pltpu.VMEM((2, PIECES, 8, 16, lane), jnp.bfloat16),
            pltpu.VMEM((2, PIECES, 8, 8, 16, lane), jnp.bfloat16),
            pltpu.VMEM((2, 5 * 128, 8 * 128), jnp.bfloat16),
            pltpu.VMEM((2, 8, 128, half), jnp.bfloat16),
            pltpu.VMEM((2, ab, half), jnp.bfloat16),
            pltpu.VMEM((2, 8, 64, ab), jnp.float32),
            pltpu.VMEM((2, 5 * 128, lane), jnp.float32),
            pltpu.VMEM((8, 64, ab), jnp.float32),
            pltpu.VMEM((NX, 8, 16, ab), jnp.float32),
            pltpu.VMEM((2, 8, 8, ab), jnp.float32),
            pltpu.VMEM((2, 8, 16, ab), jnp.float32),
            pltpu.VMEM((8, 16, ab), jnp.bfloat16),
            dma((1,)),
            dma((2,)),
            dma((2, 7)),
            dma((2, 7)),
            dma((2, 2, 4, PIECES)),
            dma((2, 2, 4, PIECES)),
            dma((2, 2, 4, PIECES)),
            dma((2, 2, 4, PIECES)),
            dma((3,)),
            dma((3,)),
            dma((3, 2)),
            dma((3, 2)),
            dma((3, 2)),
            dma((3, 2)),
        ],
        compiler_params=pltpu.CompilerParams(
            collective_id=0, has_side_effects=True, vmem_limit_bytes=55040 * 1024
        ),
        cost_estimate=pl.CostEstimate(
            flops=2 * 1024 * ab * depth, bytes_accessed=2 * ab * depth, transcendentals=0
        ),
    )(
        amplitudes,
        integrals,
        (block_size * 64 + block_owner).reshape(1, n_blocks),
    )


def solution(mesh):
    in_specs = (P("pair", "ctr"), P("pair", "ctr"), P(), P())
    return jax.shard_map(
        on_device, mesh=mesh, in_specs=in_specs, out_specs=P("ctr", "pair"), check_vma=False
    )
```

```python
import functools

import jax
import jax.numpy as jnp
import numpy as np
from jax import lax
from jax.experimental import pallas as pl
from jax.experimental.pallas import tpu as pltpu
from jax.sharding import PartitionSpec as P

MESH = pl.DeviceIdType.MESH
NY = 8
NZ = 8
NX = 4
CAP = 24
PIECES = 3
OFFS = (0, -1, 1, -2, 2, -3, 3, -4)
GROUPS = ((0, 2), (2, 6), (6, 8))


def ring_distance(d):
    d = d % 8
    return min(d, 8 - d)


def order_tables():
    first, second, names = [], [], []
    for delta in range(8):
        order = sorted(range(8), key=lambda o: (max(ring_distance(o), ring_distance(o - delta)), o))
        done = [max(ring_distance(o), ring_distance(o - delta)) for o in order]
        assert done[1] <= 2 and done[5] <= 3
        first.append(sum(order.index(OFFS[s] % 8) * 8**s for s in range(8)))
        second.append(sum(order.index((delta + OFFS[s]) % 8) * 8**s for s in range(8)))
        names.append(sum(order[i] * 8**i for i in range(8)))
    return first, second, names


def pick(table, delta):
    total = 0
    for d in range(8):
        total = total + table[d] * (1 - lax.div(lax.rem(delta - d + 8, 8) + 7, 8))
    return total


def digit(packed, i):
    return lax.rem(lax.div(packed, 8**i), 8)


def iota(shape, dim):
    return lax.broadcasted_iota(jnp.int32, shape, dim)


def kernel(
    a_hbm, b_hbm, table_ref, out_ref,
    a_ref, msg, got, sel, blocks, b_ref, acc, early, from_core, sums, from_opposite, from_x, final,
    in_sem, b_sem, send0, recv0, send1, recv1, send2, recv2, send_c, recv_c, send_o, recv_o, send_x, recv_x,
):
    pair = lax.axis_index("pair")
    ctr = lax.axis_index("ctr")
    y, z = lax.div(pair, NZ), lax.rem(pair, NZ)
    x, core = lax.div(ctr, 2), lax.rem(ctr, 2)
    delta = lax.rem(y - z + 8, 8)
    half = a_ref.shape[1] // 2
    lane = got.shape[-1]
    piece = half // PIECES
    parts = piece // lane

    def along(axis, d):
        if axis == "y":
            return (lax.rem(y + d + NY, NY) * NZ + z, ctr)
        return (y * NZ + lax.rem(z + d + NZ, NZ), ctr)

    other_core = (pair, ctr + 1 - 2 * core)

    def along_x(d):
        return (pair, lax.rem(x + d, NX) * 2 + core)

    load_a = pltpu.make_async_copy(a_hbm, a_ref, in_sem.at[0])
    load_a.start()

    barrier = pltpu.get_barrier_semaphore()
    peers = [along("y", d) for d in range(1, 8)] + [along("z", d) for d in range(1, 8)]
    peers += [other_core] + [along_x(1), along_x(3)]
    for peer in peers:
        pl.semaphore_signal(barrier, inc=1, device_id=peer, device_id_type=MESH)

    sends = []

    def send(src, dst, send_sem, recv_sem, device):
        copy = pltpu.make_async_remote_copy(
            src_ref=src, dst_ref=dst, send_sem=send_sem, recv_sem=recv_sem,
            device_id=device, device_id_type=MESH,
        )
        copy.start()
        sends.append(copy)
        return copy

    def drain(count):
        for copy in sends[:count]:
            copy.wait_send()
        del sends[:count]

    size_row = (table_ref[...] >> 6).astype(jnp.float32)
    owner_row = (table_ref[...] & 63).astype(jnp.float32)
    n_block = size_row.shape[1]
    rows, cols = iota((n_block, n_block), 0), iota((n_block, n_block), 1)
    zero = jnp.zeros((n_block, n_block), jnp.float32)
    size_col = jnp.sum(jnp.where(rows == cols, size_row + zero, 0.0), axis=1, keepdims=True)
    owner_col = jnp.sum(jnp.where(rows == cols, owner_row + zero, 0.0), axis=1, keepdims=True)
    offset_col = jnp.sum(jnp.where(cols < rows, size_row + zero, 0.0), axis=1, keepdims=True)

    mine = owner_col == pair.astype(jnp.float32)
    my_offset = jnp.sum(jnp.where(mine, offset_col, 0.0), axis=0, keepdims=True).astype(jnp.int32)
    n_msg = 8 * 16
    at = iota((n_msg, CAP), 0)
    slot = iota((n_msg, CAP), 1)
    wanted = jnp.where(
        ((slot + my_offset) & 7) == (at >> 4), (at & 15) - parts * (slot >> 3), -1
    )
    choose = [jnp.where(wanted == q, 1.0, 0.0).astype(jnp.bfloat16) for q in range(parts)]
    load_a.wait()
    loads = []
    for h in range(2):
        load = pltpu.make_async_copy(b_hbm.at[:, pl.ds(h * half, half)], b_ref.at[h], b_sem.at[h])
        load.start()
        loads.append(load)

    for h in range(2):
        for a in range(PIECES):
            total = jnp.zeros((n_msg, lane), jnp.float32)
            for q in range(parts):
                start = h * half + a * piece + q * lane
                total += jnp.dot(
                    choose[q], a_ref[:, start : start + lane], preferred_element_type=jnp.float32
                )
            msg[h, a] = total.astype(jnp.bfloat16).reshape(8, 16, lane)

    pl.semaphore_wait(barrier, len(peers))

    phase0 = []
    for d in range(1, 8):
        for h, axis, me in ((0, "z", z), (1, "y", y)):
            phase0.append(
                send(
                    msg.at[h, :, lax.rem(me + d, 8)], got.at[h, :, 0, me],
                    send0.at[h, d - 1], recv0.at[h, d - 1], along(axis, d),
                )
            )
    for a in range(PIECES):
        got[0, a, 0, z] = msg[0, a, z]
        got[1, a, 0, y] = msg[1, a, y]

    width = got.shape[2] * n_msg
    place = iota((1, width), 1)
    slot_of = place >> 7
    source = (place >> 4) & 7
    m = place & 15
    i = jnp.where(m >= parts, 1, 0) + jnp.where(m >= 2 * parts, 1, 0) + jnp.where(m >= 3 * parts, 1, 0)
    q = m - parts * i
    step = (slot_of + 1) >> 1
    ring = jnp.where((slot_of & 1) == 0, step, 8 - step)

    targets = []
    for h in range(2):
        if h == 0:
            owner = ((ring + y) & 7) * NZ + source
            cls = z
        else:
            owner = source * NZ + ((ring + z) & 7)
            cls = y
        hit = owner_col == owner.astype(jnp.float32)
        first = jnp.sum(jnp.where(hit, offset_col, 0.0), axis=0, keepdims=True).astype(jnp.int32)
        count = jnp.sum(jnp.where(hit, size_col, 0.0), axis=0, keepdims=True).astype(jnp.int32)
        k = ((first - cls + 7) >> 3) + i
        good = (8 * k + cls < first + count) & (i < 3)
        target = q * 128 + ((k >> 4) & 1) * 64 + (k >> 5) * 16 + (k & 15)
        targets.append(jnp.where(good, target, -1))

    def select(h):
        def fill(part, carry):
            row = iota((128, width), 0) + part * 128
            sel[h, pl.ds(part * 128, 128)] = jnp.where(row == targets[h], 1.0, 0.0).astype(jnp.bfloat16)
            return carry

        lax.fori_loop(0, parts, fill, 0)

    select(0)
    for copy in phase0:
        copy.wait_recv()

    lanes = (("y", "z"), ("z", "y"))

    def ring_send(view, n_rows, h, a, way, step, send_sem, recv_sem, axis):
        src = 0 if step == 0 else 2 * step - 1 + way
        dst = 7 if step == 3 else 2 * step + 1 + way
        rows = pl.ds(0, n_rows) if step < 3 else pl.ds(way * (n_rows // 2), n_rows // 2)
        return send(
            view(h, a, src, rows), view(h, a, dst, rows),
            send_sem.at[h, way, step, a], recv_sem.at[h, way, step, a],
            along(axis, 1 if way == 0 else -1),
        )

    flying1, flying2 = {}, {}

    def first_ring(step, a, h, way):
        flying1[step, a, h, way] = ring_send(
            lambda h, a, slot, rows: got.at[h, pl.ds(a, 1 if a == 0 else PIECES - 1), slot, rows], 8,
            h, a, way, step, send1, recv1, lanes[h][0],
        )

    def second_ring(step, a, h, way):
        flying2[step, a, h, way] = ring_send(
            lambda h, a, slot, rows: blocks.at[h, slot, rows, pl.ds(a * piece, piece)], 128,
            h, a, way, step, send2, recv2, lanes[h][1],
        )

    both = [(h, way) for way in range(2) for h in range(2)]
    for a in range(2):
        for h, way in both:
            first_ring(0, a, h, way)
    select(1)
    for step in range(3):
        for a in range(2):
            for h, way in both:
                flying1[step, a, h, way].wait_recv()
                first_ring(step + 1, a, h, way)
            if step == 2 and a == 0:
                for h in range(2):
                    early[h] += jnp.dot(
                        sel[h, :, 5 * n_msg : 7 * n_msg], got[h, 0, 5:7].reshape(2 * n_msg, lane),
                        preferred_element_type=jnp.float32,
                    )
        if step == 1:
            for h in range(2):
                early[h] = jnp.dot(
                    sel[h, :, : 5 * n_msg], got[h, 0, :5].reshape(5 * n_msg, lane),
                    preferred_element_type=jnp.float32,
                )

    n_early = len(sends)

    for a in range(2):
        for h in range(2):
            for way in range(2):
                flying1[3, a, h, way].wait_recv()
            if a == 0:
                value = early[h] + jnp.dot(
                    sel[h, :, 7 * n_msg :], got[h, 0, 7].reshape(n_msg, lane),
                    preferred_element_type=jnp.float32,
                )
            else:
                packed = [got[h, n].reshape(width, lane) for n in range(1, PIECES)]
                value = jnp.dot(
                    sel[h], jnp.concatenate(packed, axis=1), preferred_element_type=jnp.float32
                )
            value = value.astype(jnp.bfloat16)
            for n in range(value.shape[1] // lane):
                for q in range(parts):
                    start = (a + n) * piece + q * lane
                    blocks[h, 0, :, start : start + lane] = value[q * 128 : q * 128 + 128, n * lane : n * lane + lane]
                for way in range(2):
                    second_ring(0, a + n, h, way)
    acc[...] = jnp.zeros_like(acc)

    first_table, second_table, name_table = order_tables()
    where_to = (pick(first_table, delta), pick(second_table, delta))
    names = pick(name_table, delta)

    def multiply(slot0, n_slot, a):
        for h in range(2):
            columns = pl.ds(a * piece, piece)
            left = blocks[h, slot0 : slot0 + n_slot, :, columns].reshape(n_slot * 128, piece)
            value = lax.dot_general(
                left, b_ref[h, :, columns], (((1,), (1,)), ((), ())), preferred_element_type=jnp.float32
            )
            for s in range(n_slot):
                pos = digit(where_to[h], slot0 + s)
                for c in range(2):
                    acc[c, pos] += value[s * 128 + c * 64 : s * 128 + c * 64 + 64]

    def arrive(step, a):
        for h, way in both:
            flying2[step, a, h, way].wait_recv()
            if step < 3:
                second_ring(step + 1, a, h, way)

    def core_send(g):
        lo, hi = GROUPS[g]
        return send(
            acc.at[1 - core, pl.ds(lo, hi - lo)], from_core.at[pl.ds(lo, hi - lo)],
            send_c.at[g], recv_c.at[g], other_core,
        )

    right, left, opposite = (lax.rem(x + d, NX) for d in (1, 3, 2))

    def x_first(g, exchanged):
        lo, hi = GROUPS[g]
        exchanged.wait_recv()
        for t in range(NX):
            sums[t, lo:hi] = acc[core, lo:hi, t * 16 : t * 16 + 16] + from_core[lo:hi, t * 16 : t * 16 + 16]
        return [
            send(
                sums.at[opposite, pl.ds(lo, hi - lo), pl.ds(w * 8, 8)], from_opposite.at[w, pl.ds(lo, hi - lo)],
                send_o.at[g, w], recv_o.at[g, w], along_x((1, 3)[w]),
            )
            for w in range(2)
        ]

    def x_second(g, copies):
        lo, hi = GROUPS[g]
        out = []
        for w, near in ((0, right), (1, left)):
            copies[w].wait_recv()
            sums[near, lo:hi, w * 8 : w * 8 + 8] += from_opposite[w, lo:hi]
            out.append(
                send(
                    sums.at[near, pl.ds(lo, hi - lo)], from_x.at[w, pl.ds(lo, hi - lo)],
                    send_x.at[g, w], recv_x.at[g, w], along_x((1, 3)[w]),
                )
            )
        return out

    def finish(g, copies):
        lo, hi = GROUPS[g]
        for copy in copies:
            copy.wait_recv()
        value = sums[x, lo:hi] + from_x[0, lo:hi] + from_x[1, lo:hi]
        final[lo:hi] = value.astype(jnp.bfloat16)

    for load in loads:
        load.wait()
    for a in range(PIECES):
        multiply(0, 1, a)
    for step in range(2):
        for a in range(PIECES):
            arrive(step, a)
            multiply(2 * step + 1, 2, a)
            if step == 0 and a == 0:
                drain(n_early)
    core_a = core_send(0)
    n_early = len(sends)
    for a in range(PIECES):
        arrive(2, a)
        if a == 0:
            x_a = x_first(0, core_a)
        multiply(5, 2, a)
        if a == 1:
            x_a = x_second(0, x_a)
    core_b = core_send(1)
    row, col = iota((128, 128), 0), iota((128, 128), 1)
    pos = col >> 4
    cls = jnp.zeros((128, 128), jnp.int32)
    for n in range(8):
        cls = jnp.where(pos == n, lax.rem(digit(names, n) + z, 8), cls)
    order = jnp.where(row == (col & 15) * 8 + cls, 1.0, 0.0).astype(jnp.bfloat16)
    for a in range(PIECES):
        arrive(3, a)
        if a == 0:
            x_b = x_first(1, core_b)
        multiply(7, 1, a)
        if a == 1:
            x_b = x_second(1, x_b)
            drain(n_early)
            finish(0, x_a)
    core_c = core_send(2)
    x_c = x_second(2, x_first(2, core_c))
    finish(1, x_b)
    drain(len(sends) - 4)
    finish(2, x_c)
    value = jnp.dot(order, final[...].reshape(128, final.shape[-1]), preferred_element_type=jnp.float32)
    out_ref[...] = value.astype(jnp.bfloat16)
    drain(len(sends))


def on_device(amplitudes, integrals, block_size, block_owner):
    slots, depth = amplitudes.shape
    ab = integrals.shape[0]
    half = depth // 2
    lane = half // PIECES // 5
    n_blocks = block_size.shape[0]
    vmem = pl.BlockSpec(memory_space=pltpu.VMEM)
    dma = pltpu.SemaphoreType.DMA
    return pl.pallas_call(
        kernel,
        out_shape=jax.ShapeDtypeStruct((128, ab), jnp.bfloat16),
        in_specs=[pl.BlockSpec(memory_space=pltpu.HBM)] * 2 + [vmem],
        out_specs=vmem,
        scratch_shapes=[
            pltpu.VMEM((slots, depth), jnp.bfloat16),
            pltpu.VMEM((2, PIECES, 8, 16, lane), jnp.bfloat16),
            pltpu.VMEM((2, PIECES, 8, 8, 16, lane), jnp.bfloat16),
            pltpu.VMEM((2, 5 * 128, 8 * 128), jnp.bfloat16),
            pltpu.VMEM((2, 8, 128, half), jnp.bfloat16),
            pltpu.VMEM((2, ab, half), jnp.bfloat16),
            pltpu.VMEM((2, 8, 64, ab), jnp.float32),
            pltpu.VMEM((2, 5 * 128, lane), jnp.float32),
            pltpu.VMEM((8, 64, ab), jnp.float32),
            pltpu.VMEM((NX, 8, 16, ab), jnp.float32),
            pltpu.VMEM((2, 8, 8, ab), jnp.float32),
            pltpu.VMEM((2, 8, 16, ab), jnp.float32),
            pltpu.VMEM((8, 16, ab), jnp.bfloat16),
            dma((1,)),
            dma((2,)),
            dma((2, 7)),
            dma((2, 7)),
            dma((2, 2, 4, PIECES)),
            dma((2, 2, 4, PIECES)),
            dma((2, 2, 4, PIECES)),
            dma((2, 2, 4, PIECES)),
            dma((3,)),
            dma((3,)),
            dma((3, 2)),
            dma((3, 2)),
            dma((3, 2)),
            dma((3, 2)),
        ],
        compiler_params=pltpu.CompilerParams(
            collective_id=0, has_side_effects=True, vmem_limit_bytes=55040 * 1024
        ),
        cost_estimate=pl.CostEstimate(
            flops=2 * 1024 * ab * depth, bytes_accessed=2 * ab * depth, transcendentals=0
        ),
    )(
        amplitudes,
        integrals,
        (block_size * 64 + block_owner).reshape(1, n_blocks),
    )


def solution(mesh):
    in_specs = (P("pair", "ctr"), P("pair", "ctr"), P(), P())
    return jax.shard_map(
        on_device, mesh=mesh, in_specs=in_specs, out_specs=P("ctr", "pair"), check_vma=False
    )
```

```python
import functools

import jax
import jax.numpy as jnp
import numpy as np
from jax import lax
from jax.experimental import pallas as pl
from jax.experimental.pallas import tpu as pltpu
from jax.sharding import PartitionSpec as P

MESH = pl.DeviceIdType.MESH
NY = 8
NZ = 8
NX = 4
CAP = 24
PIECES = 3
OFFS = (0, -1, 1, -2, 2, -3, 3, -4)
GROUPS = ((0, 2), (2, 6), (6, 8))


def ring_distance(d):
    d = d % 8
    return min(d, 8 - d)


def order_tables():
    first, second, names = [], [], []
    for delta in range(8):
        order = sorted(range(8), key=lambda o: (max(ring_distance(o), ring_distance(o - delta)), o))
        done = [max(ring_distance(o), ring_distance(o - delta)) for o in order]
        assert done[1] <= 2 and done[5] <= 3
        first.append(sum(order.index(OFFS[s] % 8) * 8**s for s in range(8)))
        second.append(sum(order.index((delta + OFFS[s]) % 8) * 8**s for s in range(8)))
        names.append(sum(order[i] * 8**i for i in range(8)))
    return first, second, names


def pick(table, delta):
    total = 0
    for d in range(8):
        total = total + table[d] * (1 - lax.div(lax.rem(delta - d + 8, 8) + 7, 8))
    return total


def digit(packed, i):
    return lax.rem(lax.div(packed, 8**i), 8)


def iota(shape, dim):
    return lax.broadcasted_iota(jnp.int32, shape, dim)


def kernel(
    a_hbm, b_hbm, table_ref, out_ref,
    a_ref, msg, got, sel, blocks, b_ref, acc, early, from_core, sums, from_opposite, from_x, final,
    in_sem, b_sem, send0, recv0, send1, recv1, send2, recv2, send_c, recv_c, send_o, recv_o, send_x, recv_x,
):
    pair = lax.axis_index("pair")
    ctr = lax.axis_index("ctr")
    y, z = lax.div(pair, NZ), lax.rem(pair, NZ)
    x, core = lax.div(ctr, 2), lax.rem(ctr, 2)
    delta = lax.rem(y - z + 8, 8)
    half = a_ref.shape[1] // 2
    lane = got.shape[-1]
    piece = half // PIECES
    parts = piece // lane

    def along(axis, d):
        if axis == "y":
            return (lax.rem(y + d + NY, NY) * NZ + z, ctr)
        return (y * NZ + lax.rem(z + d + NZ, NZ), ctr)

    other_core = (pair, ctr + 1 - 2 * core)

    def along_x(d):
        return (pair, lax.rem(x + d, NX) * 2 + core)

    load_a = pltpu.make_async_copy(a_hbm, a_ref, in_sem.at[0])
    load_a.start()

    barrier = pltpu.get_barrier_semaphore()
    peers = [along("y", d) for d in range(1, 8)] + [along("z", d) for d in range(1, 8)]
    peers += [other_core] + [along_x(d) for d in (1, 2, 3)]
    for peer in peers:
        pl.semaphore_signal(barrier, inc=1, device_id=peer, device_id_type=MESH)

    sends = []

    def send(src, dst, send_sem, recv_sem, device):
        copy = pltpu.make_async_remote_copy(
            src_ref=src, dst_ref=dst, send_sem=send_sem, recv_sem=recv_sem,
            device_id=device, device_id_type=MESH,
        )
        copy.start()
        sends.append(copy)
        return copy

    def drain(count):
        for copy in sends[:count]:
            copy.wait_send()
        del sends[:count]

    size_row = (table_ref[...] >> 6).astype(jnp.float32)
    owner_row = (table_ref[...] & 63).astype(jnp.float32)
    n_block = size_row.shape[1]
    rows, cols = iota((n_block, n_block), 0), iota((n_block, n_block), 1)
    zero = jnp.zeros((n_block, n_block), jnp.float32)
    size_col = jnp.sum(jnp.where(rows == cols, size_row + zero, 0.0), axis=1, keepdims=True)
    owner_col = jnp.sum(jnp.where(rows == cols, owner_row + zero, 0.0), axis=1, keepdims=True)
    offset_col = jnp.sum(jnp.where(cols < rows, size_row + zero, 0.0), axis=1, keepdims=True)

    mine = owner_col == pair.astype(jnp.float32)
    my_offset = jnp.sum(jnp.where(mine, offset_col, 0.0), axis=0, keepdims=True).astype(jnp.int32)
    n_msg = 8 * 16
    at = iota((n_msg, CAP), 0)
    slot = iota((n_msg, CAP), 1)
    wanted = jnp.where(
        ((slot + my_offset) & 7) == (at >> 4), (at & 15) - parts * (slot >> 3), -1
    )
    choose = [jnp.where(wanted == q, 1.0, 0.0).astype(jnp.bfloat16) for q in range(parts)]
    load_a.wait()
    loads = []
    for h in range(2):
        load = pltpu.make_async_copy(b_hbm.at[:, pl.ds(h * half, half)], b_ref.at[h], b_sem.at[h])
        load.start()
        loads.append(load)

    for h in range(2):
        for a in range(PIECES):
            total = jnp.zeros((n_msg, lane), jnp.float32)
            for q in range(parts):
                start = h * half + a * piece + q * lane
                total += jnp.dot(
                    choose[q], a_ref[:, start : start + lane], preferred_element_type=jnp.float32
                )
            msg[h, a] = total.astype(jnp.bfloat16).reshape(8, 16, lane)

    pl.semaphore_wait(barrier, len(peers))

    phase0 = []
    for d in (4, 3, 5, 2, 6, 1, 7):
        for h, axis, me in ((0, "z", z), (1, "y", y)):
            phase0.append(
                send(
                    msg.at[h, :, lax.rem(me + d, 8)], got.at[h, :, 0, me],
                    send0.at[h, d - 1], recv0.at[h, d - 1], along(axis, d),
                )
            )
    for a in range(PIECES):
        got[0, a, 0, z] = msg[0, a, z]
        got[1, a, 0, y] = msg[1, a, y]

    width = got.shape[2] * n_msg
    place = iota((1, width), 1)
    slot_of = place >> 7
    source = (place >> 4) & 7
    m = place & 15
    i = jnp.where(m >= parts, 1, 0) + jnp.where(m >= 2 * parts, 1, 0) + jnp.where(m >= 3 * parts, 1, 0)
    q = m - parts * i
    step = (slot_of + 1) >> 1
    ring = jnp.where((slot_of & 1) == 0, step, 8 - step)

    targets = []
    for h in range(2):
        if h == 0:
            owner = ((ring + y) & 7) * NZ + source
            cls = z
        else:
            owner = source * NZ + ((ring + z) & 7)
            cls = y
        hit = owner_col == owner.astype(jnp.float32)
        first = jnp.sum(jnp.where(hit, offset_col, 0.0), axis=0, keepdims=True).astype(jnp.int32)
        count = jnp.sum(jnp.where(hit, size_col, 0.0), axis=0, keepdims=True).astype(jnp.int32)
        k = ((first - cls + 7) >> 3) + i
        good = (8 * k + cls < first + count) & (i < 3)
        target = q * 128 + ((k >> 4) & 1) * 64 + (k >> 5) * 16 + (k & 15)
        targets.append(jnp.where(good, target, -1))

    def select(h):
        def fill(part, carry):
            row = iota((128, width), 0) + part * 128
            sel[h, pl.ds(part * 128, 128)] = jnp.where(row == targets[h], 1.0, 0.0).astype(jnp.bfloat16)
            return carry

        lax.fori_loop(0, parts, fill, 0)

    for copy in phase0:
        copy.wait_recv()

    lanes = (("y", "z"), ("z", "y"))

    def ring_send(view, n_rows, h, a, way, step, send_sem, recv_sem, axis):
        src = 0 if step == 0 else 2 * step - 1 + way
        dst = 7 if step == 3 else 2 * step + 1 + way
        rows = pl.ds(0, n_rows) if step < 3 else pl.ds(way * (n_rows // 2), n_rows // 2)
        return send(
            view(h, a, src, rows), view(h, a, dst, rows),
            send_sem.at[h, way, step, a], recv_sem.at[h, way, step, a],
            along(axis, 1 if way == 0 else -1),
        )

    flying1, flying2 = {}, {}

    def first_ring(step, a, h, way):
        flying1[step, a, h, way] = ring_send(
            lambda h, a, slot, rows: got.at[h, a, slot, rows], 8,
            h, a, way, step, send1, recv1, lanes[h][0],
        )

    def second_ring(step, a, h, way):
        flying2[step, a, h, way] = ring_send(
            lambda h, a, slot, rows: blocks.at[h, slot, rows, pl.ds(a * piece, piece)], 128,
            h, a, way, step, send2, recv2, lanes[h][1],
        )

    both = [(h, way) for way in range(2) for h in range(2)]
    for a in range(PIECES):
        for h, way in both:
            first_ring(0, a, h, way)
    select(0)
    acc[...] = jnp.zeros_like(acc)
    for step in range(3):
        for a in range(PIECES):
            for h, way in both:
                flying1[step, a, h, way].wait_recv()
                first_ring(step + 1, a, h, way)
            if step == 2 and a == 0:
                for h in range(2):
                    early[h] += jnp.dot(
                        sel[h, :, 5 * n_msg : 7 * n_msg], got[h, 0, 5:7].reshape(2 * n_msg, lane),
                        preferred_element_type=jnp.float32,
                    )
        if step == 0:
            select(1)
        if step == 1:
            for h in range(2):
                early[h] = jnp.dot(
                    sel[h, :, : 5 * n_msg], got[h, 0, :5].reshape(5 * n_msg, lane),
                    preferred_element_type=jnp.float32,
                )

    n_early = len(sends)

    for a in range(PIECES):
        for h in range(2):
            for way in range(2):
                flying1[3, a, h, way].wait_recv()
            if a == 0:
                value = early[h] + jnp.dot(
                    sel[h, :, 7 * n_msg :], got[h, 0, 7].reshape(n_msg, lane),
                    preferred_element_type=jnp.float32,
                )
            else:
                value = jnp.dot(
                    sel[h], got[h, a].reshape(width, lane), preferred_element_type=jnp.float32
                )
            value = value.astype(jnp.bfloat16)
            for q in range(parts):
                start = a * piece + q * lane
                blocks[h, 0, :, start : start + lane] = value[q * 128 : q * 128 + 128]
            for way in range(2):
                second_ring(0, a, h, way)

    first_table, second_table, name_table = order_tables()
    where_to = (pick(first_table, delta), pick(second_table, delta))
    names = pick(name_table, delta)

    def multiply(slot0, n_slot, a):
        for h in range(2):
            columns = pl.ds(a * piece, piece)
            left = blocks[h, slot0 : slot0 + n_slot, :, columns].reshape(n_slot * 128, piece)
            value = lax.dot_general(
                left, b_ref[h, :, columns], (((1,), (1,)), ((), ())), preferred_element_type=jnp.float32
            )
            for s in range(n_slot):
                pos = digit(where_to[h], slot0 + s)
                for c in range(2):
                    acc[c, pos] += value[s * 128 + c * 64 : s * 128 + c * 64 + 64]

    def arrive(step, a):
        for h, way in both:
            flying2[step, a, h, way].wait_recv()
            if step < 3:
                second_ring(step + 1, a, h, way)

    def core_send(g):
        lo, hi = GROUPS[g]
        return send(
            acc.at[1 - core, pl.ds(lo, hi - lo)], from_core.at[pl.ds(lo, hi - lo)],
            send_c.at[g], recv_c.at[g], other_core,
        )

    right, left, opposite = (lax.rem(x + d, NX) for d in (1, 3, 2))

    def add_cores(g, exchanged):
        lo, hi = GROUPS[g]
        exchanged.wait_recv()
        for t in range(NX):
            sums[t, lo:hi] = acc[core, lo:hi, t * 16 : t * 16 + 16] + from_core[lo:hi, t * 16 : t * 16 + 16]

    def x_direct(g, exchanged):
        lo, hi = GROUPS[g]
        add_cores(g, exchanged)
        return [
            send(
                sums.at[lax.rem(x + d, NX), pl.ds(lo, hi - lo)], from_x.at[w, pl.ds(lo, hi - lo)],
                send_x.at[g, w], recv_x.at[g, w], along_x(d),
            )
            for w, d in ((2, 2), (0, 1), (1, 3))
        ]

    def x_first(g, exchanged):
        lo, hi = GROUPS[g]
        add_cores(g, exchanged)
        return [
            send(
                sums.at[opposite, pl.ds(lo, hi - lo), pl.ds(w * 8, 8)], from_opposite.at[w, pl.ds(lo, hi - lo)],
                send_o.at[g, w], recv_o.at[g, w], along_x((1, 3)[w]),
            )
            for w in range(2)
        ]

    def x_second(g, copies):
        lo, hi = GROUPS[g]
        out = []
        for w, near in ((0, right), (1, left)):
            copies[w].wait_recv()
            sums[near, lo:hi, w * 8 : w * 8 + 8] += from_opposite[w, lo:hi]
            out.append(
                send(
                    sums.at[near, pl.ds(lo, hi - lo)], from_x.at[w, pl.ds(lo, hi - lo)],
                    send_x.at[g, w], recv_x.at[g, w], along_x((1, 3)[w]),
                )
            )
        return out

    def finish(g, copies):
        lo, hi = GROUPS[g]
        for copy in copies:
            copy.wait_recv()
        value = sums[x, lo:hi] + from_x[0, lo:hi] + from_x[1, lo:hi]
        if len(copies) == 3:
            value += from_x[2, lo:hi]
        final[lo:hi] = value.astype(jnp.bfloat16)

    for load in loads:
        load.wait()
    for a in range(PIECES):
        multiply(0, 1, a)
    for step in range(2):
        for a in range(PIECES):
            arrive(step, a)
            multiply(2 * step + 1, 2, a)
            if step == 0 and a == 0:
                drain(n_early)
    core_a = core_send(0)
    n_early = len(sends)
    for a in range(PIECES):
        arrive(2, a)
        if a == 0:
            x_a = x_first(0, core_a)
        multiply(5, 2, a)
        if a == 1:
            x_a = x_second(0, x_a)
    core_b = core_send(1)
    row, col = iota((128, 128), 0), iota((128, 128), 1)
    pos = col >> 4
    cls = jnp.zeros((128, 128), jnp.int32)
    for n in range(8):
        cls = jnp.where(pos == n, lax.rem(digit(names, n) + z, 8), cls)
    order = jnp.where(row == (col & 15) * 8 + cls, 1.0, 0.0).astype(jnp.bfloat16)
    for a in range(PIECES):
        arrive(3, a)
        if a == 0:
            x_b = x_first(1, core_b)
        multiply(7, 1, a)
        if a == 1:
            x_b = x_second(1, x_b)
            drain(n_early)
            finish(0, x_a)
    core_c = core_send(2)
    x_c = x_direct(2, core_c)
    finish(1, x_b)
    drain(len(sends) - 3)
    finish(2, x_c)
    value = jnp.dot(order, final[...].reshape(128, final.shape[-1]), preferred_element_type=jnp.float32)
    out_ref[...] = value.astype(jnp.bfloat16)
    drain(len(sends))


def on_device(amplitudes, integrals, block_size, block_owner):
    slots, depth = amplitudes.shape
    ab = integrals.shape[0]
    half = depth // 2
    lane = half // PIECES // 5
    n_blocks = block_size.shape[0]
    vmem = pl.BlockSpec(memory_space=pltpu.VMEM)
    dma = pltpu.SemaphoreType.DMA
    return pl.pallas_call(
        kernel,
        out_shape=jax.ShapeDtypeStruct((128, ab), jnp.bfloat16),
        in_specs=[pl.BlockSpec(memory_space=pltpu.HBM)] * 2 + [vmem],
        out_specs=vmem,
        scratch_shapes=[
            pltpu.VMEM((slots, depth), jnp.bfloat16),
            pltpu.VMEM((2, PIECES, 8, 16, lane), jnp.bfloat16),
            pltpu.VMEM((2, PIECES, 8, 8, 16, lane), jnp.bfloat16),
            pltpu.VMEM((2, 5 * 128, 8 * 128), jnp.bfloat16),
            pltpu.VMEM((2, 8, 128, half), jnp.bfloat16),
            pltpu.VMEM((2, ab, half), jnp.bfloat16),
            pltpu.VMEM((2, 8, 64, ab), jnp.float32),
            pltpu.VMEM((2, 5 * 128, lane), jnp.float32),
            pltpu.VMEM((8, 64, ab), jnp.float32),
            pltpu.VMEM((NX, 8, 16, ab), jnp.float32),
            pltpu.VMEM((2, 8, 8, ab), jnp.float32),
            pltpu.VMEM((3, 8, 16, ab), jnp.float32),
            pltpu.VMEM((8, 16, ab), jnp.bfloat16),
            dma((1,)),
            dma((2,)),
            dma((2, 7)),
            dma((2, 7)),
            dma((2, 2, 4, PIECES)),
            dma((2, 2, 4, PIECES)),
            dma((2, 2, 4, PIECES)),
            dma((2, 2, 4, PIECES)),
            dma((3,)),
            dma((3,)),
            dma((3, 2)),
            dma((3, 2)),
            dma((3, 3)),
            dma((3, 3)),
        ],
        compiler_params=pltpu.CompilerParams(
            collective_id=0, has_side_effects=True, vmem_limit_bytes=55040 * 1024
        ),
        cost_estimate=pl.CostEstimate(
            flops=2 * 1024 * ab * depth, bytes_accessed=2 * ab * depth, transcendentals=0
        ),
    )(
        amplitudes,
        integrals,
        (block_size * 64 + block_owner).reshape(1, n_blocks),
    )


def solution(mesh):
    in_specs = (P("pair", "ctr"), P("pair", "ctr"), P(), P())
    return jax.shard_map(
        on_device, mesh=mesh, in_specs=in_specs, out_specs=P("ctr", "pair"), check_vma=False
    )
```

```python
import functools

import jax
import jax.numpy as jnp
import numpy as np
from jax import lax
from jax.experimental import pallas as pl
from jax.experimental.pallas import tpu as pltpu
from jax.sharding import PartitionSpec as P

MESH = pl.DeviceIdType.MESH
NY = 8
NZ = 8
NX = 4
CAP = 24
PIECES = 3
OFFS = (0, -1, 1, -2, 2, -3, 3, -4)
GROUPS = ((0, 2), (2, 6), (6, 8))


def ring_distance(d):
    d = d % 8
    return min(d, 8 - d)


def order_tables():
    first, second, names = [], [], []
    for delta in range(8):
        order = sorted(range(8), key=lambda o: (max(ring_distance(o), ring_distance(o - delta)), o))
        done = [max(ring_distance(o), ring_distance(o - delta)) for o in order]
        assert done[1] <= 2 and done[5] <= 3
        first.append(sum(order.index(OFFS[s] % 8) * 8**s for s in range(8)))
        second.append(sum(order.index((delta + OFFS[s]) % 8) * 8**s for s in range(8)))
        names.append(sum(order[i] * 8**i for i in range(8)))
    return first, second, names


def pick(table, delta):
    total = 0
    for d in range(8):
        total = total + table[d] * (1 - lax.div(lax.rem(delta - d + 8, 8) + 7, 8))
    return total


def digit(packed, i):
    return lax.rem(lax.div(packed, 8**i), 8)


def iota(shape, dim):
    return lax.broadcasted_iota(jnp.int32, shape, dim)


def kernel(
    a_hbm, b_hbm, table_ref, out_ref,
    a_ref, msg, got, sel, blocks, b_ref, acc, early, from_core, sums, from_opposite, from_x, final,
    in_sem, b_sem, send0, recv0, send1, recv1, send2, recv2, send_c, recv_c, send_o, recv_o, send_x, recv_x,
):
    pair = lax.axis_index("pair")
    ctr = lax.axis_index("ctr")
    y, z = lax.div(pair, NZ), lax.rem(pair, NZ)
    x, core = lax.div(ctr, 2), lax.rem(ctr, 2)
    delta = lax.rem(y - z + 8, 8)
    half = a_ref.shape[1] // 2
    lane = got.shape[-1]
    piece = half // PIECES
    parts = piece // lane

    def along(axis, d):
        if axis == "y":
            return (lax.rem(y + d + NY, NY) * NZ + z, ctr)
        return (y * NZ + lax.rem(z + d + NZ, NZ), ctr)

    other_core = (pair, ctr + 1 - 2 * core)

    def along_x(d):
        return (pair, lax.rem(x + d, NX) * 2 + core)

    load_a = pltpu.make_async_copy(a_hbm, a_ref, in_sem.at[0])
    load_a.start()

    barrier = pltpu.get_barrier_semaphore()
    peers = [along("y", d) for d in range(1, 8)] + [along("z", d) for d in range(1, 8)]
    peers += [other_core] + [along_x(d) for d in (1, 2, 3)]
    for peer in peers:
        pl.semaphore_signal(barrier, inc=1, device_id=peer, device_id_type=MESH)

    sends = []

    def send(src, dst, send_sem, recv_sem, device):
        copy = pltpu.make_async_remote_copy(
            src_ref=src, dst_ref=dst, send_sem=send_sem, recv_sem=recv_sem,
            device_id=device, device_id_type=MESH,
        )
        copy.start()
        sends.append(copy)
        return copy

    def drain(count):
        for copy in sends[:count]:
            copy.wait_send()
        del sends[:count]

    size_row = (table_ref[...] >> 6).astype(jnp.float32)
    owner_row = (table_ref[...] & 63).astype(jnp.float32)
    n_block = size_row.shape[1]
    rows, cols = iota((n_block, n_block), 0), iota((n_block, n_block), 1)
    zero = jnp.zeros((n_block, n_block), jnp.float32)
    size_col = jnp.sum(jnp.where(rows == cols, size_row + zero, 0.0), axis=1, keepdims=True)
    owner_col = jnp.sum(jnp.where(rows == cols, owner_row + zero, 0.0), axis=1, keepdims=True)
    offset_col = jnp.sum(jnp.where(cols < rows, size_row + zero, 0.0), axis=1, keepdims=True)

    mine = owner_col == pair.astype(jnp.float32)
    my_offset = jnp.sum(jnp.where(mine, offset_col, 0.0), axis=0, keepdims=True).astype(jnp.int32)
    n_msg = 8 * 16
    at = iota((n_msg, CAP), 0)
    slot = iota((n_msg, CAP), 1)
    wanted = jnp.where(
        ((slot + my_offset) & 7) == (at >> 4), (at & 15) - parts * (slot >> 3), -1
    )
    choose = [jnp.where(wanted == q, 1.0, 0.0).astype(jnp.bfloat16) for q in range(parts)]
    load_a.wait()
    loads = []
    for h in range(2):
        load = pltpu.make_async_copy(b_hbm.at[:, pl.ds(h * half, half)], b_ref.at[h], b_sem.at[h])
        load.start()
        loads.append(load)

    for h in range(2):
        for a in range(PIECES):
            total = jnp.zeros((n_msg, lane), jnp.float32)
            for q in range(parts):
                start = h * half + a * piece + q * lane
                total += jnp.dot(
                    choose[q], a_ref[:, start : start + lane], preferred_element_type=jnp.float32
                )
            msg[h, a] = total.astype(jnp.bfloat16).reshape(8, 16, lane)

    pl.semaphore_wait(barrier, len(peers))

    phase0 = []
    for d in (4, 3, 5, 2, 6, 1, 7):
        for h, axis, me in ((0, "z", z), (1, "y", y)):
            phase0.append(
                send(
                    msg.at[h, :, lax.rem(me + d, 8)], got.at[h, :, 0, me],
                    send0.at[h, d - 1], recv0.at[h, d - 1], along(axis, d),
                )
            )
    for a in range(PIECES):
        got[0, a, 0, z] = msg[0, a, z]
        got[1, a, 0, y] = msg[1, a, y]

    width = got.shape[2] * n_msg
    place = iota((1, width), 1)
    slot_of = place >> 7
    source = (place >> 4) & 7
    m = place & 15
    i = jnp.where(m >= parts, 1, 0) + jnp.where(m >= 2 * parts, 1, 0) + jnp.where(m >= 3 * parts, 1, 0)
    q = m - parts * i
    step = (slot_of + 1) >> 1
    ring = jnp.where((slot_of & 1) == 0, step, 8 - step)

    targets = []
    for h in range(2):
        if h == 0:
            owner = ((ring + y) & 7) * NZ + source
            cls = z
        else:
            owner = source * NZ + ((ring + z) & 7)
            cls = y
        hit = owner_col == owner.astype(jnp.float32)
        first = jnp.sum(jnp.where(hit, offset_col, 0.0), axis=0, keepdims=True).astype(jnp.int32)
        count = jnp.sum(jnp.where(hit, size_col, 0.0), axis=0, keepdims=True).astype(jnp.int32)
        k = ((first - cls + 7) >> 3) + i
        good = (8 * k + cls < first + count) & (i < 3)
        target = q * 128 + ((k >> 4) & 1) * 64 + (k >> 5) * 16 + (k & 15)
        targets.append(jnp.where(good, target, -1))

    def select(h):
        def fill(part, carry):
            row = iota((128, width), 0) + part * 128
            sel[h, pl.ds(part * 128, 128)] = jnp.where(row == targets[h], 1.0, 0.0).astype(jnp.bfloat16)
            return carry

        lax.fori_loop(0, parts, fill, 0)

    for copy in phase0:
        copy.wait_recv()

    lanes = (("y", "z"), ("z", "y"))

    def ring_send(view, n_rows, h, a, way, step, send_sem, recv_sem, axis):
        src = 0 if step == 0 else 2 * step - 1 + way
        dst = 7 if step == 3 else 2 * step + 1 + way
        rows = pl.ds(0, n_rows) if step < 3 else pl.ds(way * (n_rows // 2), n_rows // 2)
        return send(
            view(h, a, src, rows), view(h, a, dst, rows),
            send_sem.at[h, way, step, a], recv_sem.at[h, way, step, a],
            along(axis, 1 if way == 0 else -1),
        )

    flying1, flying2 = {}, {}

    def first_ring(step, a, h, way):
        flying1[step, a, h, way] = ring_send(
            lambda h, a, slot, rows: got.at[h, a, slot, rows], 8,
            h, a, way, step, send1, recv1, lanes[h][0],
        )

    def second_ring(step, a, h, way):
        flying2[step, a, h, way] = ring_send(
            lambda h, a, slot, rows: blocks.at[h, slot, rows, pl.ds(a * piece, piece)], 128,
            h, a, way, step, send2, recv2, lanes[h][1],
        )

    both = [(h, way) for way in range(2) for h in range(2)]
    for a in range(PIECES):
        for h, way in both:
            first_ring(0, a, h, way)
    select(0)
    acc[...] = jnp.zeros_like(acc)
    for step in range(3):
        for a in range(PIECES):
            for h, way in both:
                flying1[step, a, h, way].wait_recv()
                first_ring(step + 1, a, h, way)
            if step == 2 and a == 0:
                for h in range(2):
                    early[h] += jnp.dot(
                        sel[h, :, 5 * n_msg : 7 * n_msg], got[h, 0, 5:7].reshape(2 * n_msg, lane),
                        preferred_element_type=jnp.float32,
                    )
        if step == 0:
            select(1)
        if step == 1:
            for h in range(2):
                early[h] = jnp.dot(
                    sel[h, :, : 5 * n_msg], got[h, 0, :5].reshape(5 * n_msg, lane),
                    preferred_element_type=jnp.float32,
                )

    n_early = len(sends)

    for a in range(PIECES):
        for h in range(2):
            for way in range(2):
                flying1[3, a, h, way].wait_recv()
            if a == 0:
                value = early[h] + jnp.dot(
                    sel[h, :, 7 * n_msg :], got[h, 0, 7].reshape(n_msg, lane),
                    preferred_element_type=jnp.float32,
                )
            else:
                value = jnp.dot(
                    sel[h], got[h, a].reshape(width, lane), preferred_element_type=jnp.float32
                )
            value = value.astype(jnp.bfloat16)
            for q in range(parts):
                start = a * piece + q * lane
                blocks[h, 0, :, start : start + lane] = value[q * 128 : q * 128 + 128]
            for way in range(2):
                second_ring(0, a, h, way)

    first_table, second_table, name_table = order_tables()
    where_to = (pick(first_table, delta), pick(second_table, delta))
    names = pick(name_table, delta)

    def multiply(slot0, n_slot, a, halves=(0, 1)):
        for h in halves:
            columns = pl.ds(a * piece, piece)
            left = blocks[h, slot0 : slot0 + n_slot, :, columns].reshape(n_slot * 128, piece)
            value = lax.dot_general(
                left, b_ref[h, :, columns], (((1,), (1,)), ((), ())), preferred_element_type=jnp.float32
            )
            for s in range(n_slot):
                pos = digit(where_to[h], slot0 + s)
                for c in range(2):
                    acc[c, pos] += value[s * 128 + c * 64 : s * 128 + c * 64 + 64]

    def arrive(step, a):
        for h, way in both:
            flying2[step, a, h, way].wait_recv()
            if step < 3:
                second_ring(step + 1, a, h, way)

    def core_send(g):
        lo, hi = GROUPS[g]
        return [core_send_at(g, lo, hi - lo)]

    def core_send_at(n, pos, count):
        return send(
            acc.at[1 - core, pl.ds(pos, count)], from_core.at[pl.ds(pos, count)],
            send_c.at[n], recv_c.at[n], other_core,
        )

    right, left, opposite = (lax.rem(x + d, NX) for d in (1, 3, 2))

    def add_cores(g, exchanged):
        lo, hi = GROUPS[g]
        for copy in exchanged:
            copy.wait_recv()
        for t in range(NX):
            sums[t, lo:hi] = acc[core, lo:hi, t * 16 : t * 16 + 16] + from_core[lo:hi, t * 16 : t * 16 + 16]

    def x_direct(g, exchanged):
        lo, hi = GROUPS[g]
        add_cores(g, exchanged)
        return [
            send(
                sums.at[lax.rem(x + d, NX), pl.ds(lo, hi - lo)], from_x.at[w, pl.ds(lo, hi - lo)],
                send_x.at[g, w], recv_x.at[g, w], along_x(d),
            )
            for w, d in ((2, 2), (0, 1), (1, 3))
        ]

    def x_first(g, exchanged):
        lo, hi = GROUPS[g]
        add_cores(g, exchanged)
        return [
            send(
                sums.at[opposite, pl.ds(lo, hi - lo), pl.ds(w * 8, 8)], from_opposite.at[w, pl.ds(lo, hi - lo)],
                send_o.at[g, w], recv_o.at[g, w], along_x((1, 3)[w]),
            )
            for w in range(2)
        ]

    def x_second(g, copies):
        lo, hi = GROUPS[g]
        out = []
        for w, near in ((0, right), (1, left)):
            copies[w].wait_recv()
            sums[near, lo:hi, w * 8 : w * 8 + 8] += from_opposite[w, lo:hi]
            out.append(
                send(
                    sums.at[near, pl.ds(lo, hi - lo)], from_x.at[w, pl.ds(lo, hi - lo)],
                    send_x.at[g, w], recv_x.at[g, w], along_x((1, 3)[w]),
                )
            )
        return out

    def finish(g, copies):
        lo, hi = GROUPS[g]
        for copy in copies:
            copy.wait_recv()
        value = sums[x, lo:hi] + from_x[0, lo:hi] + from_x[1, lo:hi]
        if len(copies) == 3:
            value += from_x[2, lo:hi]
        final[lo:hi] = value.astype(jnp.bfloat16)

    for load in loads:
        load.wait()
    for a in range(PIECES):
        multiply(0, 1, a)
    for step in range(2):
        for a in range(PIECES):
            arrive(step, a)
            multiply(2 * step + 1, 2, a)
            if step == 0 and a == 0:
                drain(n_early)
    core_a = core_send(0)
    n_early = len(sends)
    for a in range(PIECES):
        arrive(2, a)
        if a == 0:
            x_a = x_direct(0, core_a)
        multiply(5, 2, a)
    core_b = core_send(1)
    row, col = iota((128, 128), 0), iota((128, 128), 1)
    pos = col >> 4
    cls = jnp.zeros((128, 128), jnp.int32)
    for n in range(8):
        cls = jnp.where(pos == n, lax.rem(digit(names, n) + z, 8), cls)
    order = jnp.where(row == (col & 15) * 8 + cls, 1.0, 0.0).astype(jnp.bfloat16)
    for a in range(PIECES):
        arrive(3, a)
        if a == 0:
            x_b = x_first(1, core_b)
        if a < 2:
            multiply(7, 1, a)
        if a == 1:
            x_b = x_second(1, x_b)
            drain(n_early)
            finish(0, x_a)
    last = digit(where_to[1], 7)
    multiply(7, 1, 2, (0,))
    core_c = [core_send_at(2, 13 - last, 1)]
    multiply(7, 1, 2, (1,))
    core_c += [core_send_at(3, last, 1)]
    x_c = x_direct(2, core_c)
    finish(1, x_b)
    drain(len(sends) - 3)
    finish(2, x_c)
    value = jnp.dot(order, final[...].reshape(128, final.shape[-1]), preferred_element_type=jnp.float32)
    out_ref[...] = value.astype(jnp.bfloat16)
    drain(len(sends))


def on_device(amplitudes, integrals, block_size, block_owner):
    slots, depth = amplitudes.shape
    ab = integrals.shape[0]
    half = depth // 2
    lane = half // PIECES // 5
    n_blocks = block_size.shape[0]
    vmem = pl.BlockSpec(memory_space=pltpu.VMEM)
    dma = pltpu.SemaphoreType.DMA
    return pl.pallas_call(
        kernel,
        out_shape=jax.ShapeDtypeStruct((128, ab), jnp.bfloat16),
        in_specs=[pl.BlockSpec(memory_space=pltpu.HBM)] * 2 + [vmem],
        out_specs=vmem,
        scratch_shapes=[
            pltpu.VMEM((slots, depth), jnp.bfloat16),
            pltpu.VMEM((2, PIECES, 8, 16, lane), jnp.bfloat16),
            pltpu.VMEM((2, PIECES, 8, 8, 16, lane), jnp.bfloat16),
            pltpu.VMEM((2, 5 * 128, 8 * 128), jnp.bfloat16),
            pltpu.VMEM((2, 8, 128, half), jnp.bfloat16),
            pltpu.VMEM((2, ab, half), jnp.bfloat16),
            pltpu.VMEM((2, 8, 64, ab), jnp.float32),
            pltpu.VMEM((2, 5 * 128, lane), jnp.float32),
            pltpu.VMEM((8, 64, ab), jnp.float32),
            pltpu.VMEM((NX, 8, 16, ab), jnp.float32),
            pltpu.VMEM((2, 8, 8, ab), jnp.float32),
            pltpu.VMEM((3, 8, 16, ab), jnp.float32),
            pltpu.VMEM((8, 16, ab), jnp.bfloat16),
            dma((1,)),
            dma((2,)),
            dma((2, 7)),
            dma((2, 7)),
            dma((2, 2, 4, PIECES)),
            dma((2, 2, 4, PIECES)),
            dma((2, 2, 4, PIECES)),
            dma((2, 2, 4, PIECES)),
            dma((4,)),
            dma((4,)),
            dma((3, 2)),
            dma((3, 2)),
            dma((3, 3)),
            dma((3, 3)),
        ],
        compiler_params=pltpu.CompilerParams(
            collective_id=0, has_side_effects=True, vmem_limit_bytes=55040 * 1024
        ),
        cost_estimate=pl.CostEstimate(
            flops=2 * 1024 * ab * depth, bytes_accessed=2 * ab * depth, transcendentals=0
        ),
    )(
        amplitudes,
        integrals,
        (block_size * 64 + block_owner).reshape(1, n_blocks),
    )


def solution(mesh):
    in_specs = (P("pair", "ctr"), P("pair", "ctr"), P(), P())
    return jax.shard_map(
        on_device, mesh=mesh, in_specs=in_specs, out_specs=P("ctr", "pair"), check_vma=False
    )
```
